32 devices in a mesh: gx: 4 (over y, x), gy: 8 (over z, core).
Axes of the slice: x: 2, y: 2, z: 4, core: 2. Of those that a mesh axis runs over, the one named last changes fastest.
Arguments:
- probes: bfloat16 [8, 64, 32, 128], P('gx', 'gy'), may hold values from -6 to 6
- leaf_basis: bfloat16 [128, 64], replicated, may hold values from -0.5 to 0.5
- up_transfer: bfloat16 [7, 4, 64, 64], replicated, may hold values from -0.375 to 0.375
- down_transfer: bfloat16 [7, 4, 64, 64], replicated, may hold values from -0.75 to 0.75
- coupling: bfloat16 [8, 40, 64, 64], replicated, may hold values from -0.15625 to 0.15625
- far_ids: int32 [8, 4, 27], replicated, may hold values from 0 to 39
Outputs:
- product: bfloat16 [8, 64, 32, 128], P('gx', 'gy')
The draws below stay inside these ranges and needn't reach their ends.
Inputs may be any that keep to these rules, and one draw needn't show every extreme that they name: `far_ids`: each entry picks one of the 40 coupling matrices of its level.
All inputs are finite; a program needn't handle non-finite values.
Results may differ from the reference program's by a relative error of at most 0.012.
Values may be sent and summed in bfloat16 or wider, within the bound.
A program may use at most 128 MiB of HBM per device.

```python
import jax
import jax.numpy as jnp
from jax import lax

LEAF_ROWS = 8
LEAF_COLS = 16
LEAF = 128
RANK = 64
PROBES = 32
LEVELS = 8
NCOUP = 40
SLOTS = 27
GX = 8
GY = 64


def set_ends(array, key, low, high):
    shape = array.shape
    spot = [jax.random.randint(jax.random.fold_in(key, axis), (), 0, shape[axis]) for axis in range(len(shape))]
    array = array.at[tuple(spot)].set(low)
    longest = shape.index(max(shape))
    spot[longest] = (spot[longest] + 1) % shape[longest]
    return array.at[tuple(spot)].set(high)


def shard_levels(key, extent, shards, smallest, top_value):
    loudness = 1.0
    for axis_at, shards_of in shards:
        heights = jax.random.uniform(jax.random.fold_in(jax.random.fold_in(key, 6), axis_at), (shards_of,), jnp.float32, smallest / len(shards), top_value / len(shards))
        loudness = loudness * jnp.repeat(jnp.exp(heights), extent[axis_at] // shards_of).reshape((-1,) + (1,) * (len(extent) - 1 - axis_at))
    return loudness


def scatter_about(key, extent, deviation, bound, shards=(), kind=jnp.bfloat16):
    array = deviation * jax.random.normal(key, extent, jnp.float32)
    if shards:
        array = array * shard_levels(key, extent, shards, -0.22, 0.18)
    return jnp.clip(array, -bound, bound).astype(kind)


def setup_inputs(seed: int = 0) -> dict:
    key_list = jax.random.split(jax.random.key(seed), 7)
    return {
        "probes": scatter_about(key_list[0], (GX, GY, PROBES, LEAF), 1.0, 6.0, ((0, 4), (1, 8))),
        "leaf_basis": scatter_about(key_list[1], (LEAF, RANK), LEAF ** -0.5, 0.5),
        "up_transfer": scatter_about(key_list[2], (LEVELS - 1, 4, RANK, RANK), (4 * RANK) ** -0.5, 0.375),
        "down_transfer": scatter_about(key_list[3], (LEVELS - 1, 4, RANK, RANK), RANK ** -0.5, 0.75),
        "coupling": scatter_about(key_list[4], (LEVELS, NCOUP, RANK, RANK), (SLOTS * RANK) ** -0.5, 0.15625),
        "far_ids": set_ends(jax.random.randint(key_list[5], (LEVELS, 4, SLOTS), 0, NCOUP), jax.random.fold_in(key_list[5], 1), 0, NCOUP - 1).astype(jnp.int32),
    }


length_scale = 1.5

def slot_offsets(type_row, type_col):
    offsets = []
    for off_row in range(-2 - type_row, 4 - type_row):
        for off_col in range(-2 - type_col, 4 - type_col):
            if max(abs(off_row), abs(off_col)) > 1:
                offsets.append((off_row, off_col))
    return offsets

def kernel_tables(rows_leaf, cols_leaf):
    points = jnp.arange(rows_leaf * cols_leaf, dtype=jnp.int32)
    point_row = (points // cols_leaf).astype(jnp.float32)
    point_col = (points % cols_leaf).astype(jnp.float32)
    tables = []
    for off_row in (-1, 0, 1):
        for off_col in (-1, 0, 1):
            apart_row = point_row[:, None] + off_row * rows_leaf - point_row[None, :]
            apart_col = point_col[:, None] + off_col * cols_leaf - point_col[None, :]
            scaled = jnp.sqrt(3.0 * (apart_row * apart_row + apart_col * apart_col)) / length_scale
            tables.append(((1.0 + scaled) * jnp.exp(-scaled)).astype(jnp.bfloat16))
    return jnp.stack(tables)

def upward(coeffs, transfer):
    rows_count, cols_count, count_p, rank_size = coeffs.shape
    padded = jnp.pad(coeffs, ((0, rows_count % 2), (0, cols_count % 2), (0, 0), (0, 0)))
    grouped = padded.reshape((rows_count + 1) // 2, 2, (cols_count + 1) // 2, 2, count_p, rank_size).astype(jnp.float32)
    parent_coef = jnp.einsum('iajbpr,abrq->ijpq', grouped, transfer.reshape(2, 2, rank_size, rank_size).astype(jnp.float32))
    return parent_coef.astype(jnp.bfloat16)

def far_field(coeffs, coupling_level, ids_level):
    rows_count, cols_count, count_p, rank_size = coeffs.shape
    padded = jnp.pad(coeffs, ((3, 3), (3, 3), (0, 0), (0, 0)))
    result = jnp.zeros((rows_count, cols_count, count_p, rank_size), jnp.float32)
    for type_row in (0, 1):
        for type_col in (0, 1):
            count_row = (rows_count - type_row + 1) // 2
            count_col = (cols_count - type_col + 1) // 2
            if count_row == 0 or count_col == 0:
                continue
            partial_value = jnp.zeros((count_row, count_col, count_p, rank_size), jnp.float32)
            for slot_index, (off_row, off_col) in enumerate(slot_offsets(type_row, type_col)):
                start_row = type_row + 3 + off_row
                start_col = type_col + 3 + off_col
                sliced = lax.slice(padded, (start_row, start_col, 0, 0), (start_row + 2 * count_row - 1, start_col + 2 * count_col - 1, count_p, rank_size), (2, 2, 1, 1))
                matrix = coupling_level[ids_level[2 * type_row + type_col, slot_index]]
                partial_value = partial_value + jnp.einsum('ijpr,rq->ijpq', sliced.astype(jnp.float32), matrix.astype(jnp.float32))
            result = result.at[type_row::2, type_col::2].set(partial_value)
    return result

def downward(parent, transfer, rows_count, cols_count):
    parent_rows, parent_cols, count_p, rank_size = parent.shape
    spread = jnp.einsum('ijpr,abrq->iajbpq', parent.astype(jnp.float32), transfer.reshape(2, 2, rank_size, rank_size).astype(jnp.float32))
    return spread.reshape(2 * parent_rows, 2 * parent_cols, count_p, rank_size)[:rows_count, :cols_count]

def reference(probes, leaf_basis, up_transfer, down_transfer, coupling, far_ids):
    grid_rows, grid_cols, count_p, leaf_size = probes.shape
    levels = coupling.shape[0]
    basis_wide = leaf_basis.astype(jnp.float32)
    first = jnp.einsum('abpq,qr->abpr', probes.astype(jnp.float32), basis_wide).astype(jnp.bfloat16)
    ladder = [first]
    for height in range(levels - 1):
        ladder.append(upward(ladder[-1], up_transfer[height]))
    carried = None
    for height in reversed(range(levels)):
        summed = far_field(ladder[height], coupling[height], far_ids[height])
        if carried is not None:
            summed = summed + downward(carried, down_transfer[height], ladder[height].shape[0], ladder[height].shape[1])
        carried = summed.astype(jnp.bfloat16)
    tables_wide = kernel_tables(LEAF_ROWS, LEAF_COLS).astype(jnp.float32)
    padded = jnp.pad(probes, ((1, 1), (1, 1), (0, 0), (0, 0)))

    def output_row(row_index):
        sliced = lax.dynamic_slice_in_dim(padded, row_index, 3, 0).astype(jnp.float32)
        summed = jnp.zeros((grid_cols, count_p, leaf_size), jnp.float32)
        for off_row in (-1, 0, 1):
            for off_col in (-1, 0, 1):
                neighbour = sliced[off_row + 1, off_col + 1:off_col + 1 + grid_cols]
                summed = summed + jnp.einsum('bpq,qr->bpr', neighbour, tables_wide[3 * (off_row + 1) + off_col + 1])
        local_row = lax.dynamic_index_in_dim(carried, row_index, 0, keepdims=False).astype(jnp.float32)
        summed = summed + jnp.einsum('bpr,qr->bpq', local_row, basis_wide)
        return summed.astype(jnp.bfloat16)
    return lax.map(output_row, jnp.arange(grid_rows, dtype=jnp.int32))
```

```python
import functools

import jax
import jax.numpy as jnp
from jax import lax
from jax.experimental import pallas as pl
from jax.experimental.pallas import tpu as pltpu
from jax.sharding import PartitionSpec as P

LEAF_ROWS = 8
LEAF_COLS = 16
LENGTH_SCALE = 1.5
MESH = pl.DeviceIdType.MESH
BF16 = jnp.bfloat16
F32 = jnp.float32
AROUND = [(du, dv) for du in (-1, 0, 1) for dv in (-1, 0, 1) if (du, dv) != (0, 0)]


def slot_offsets(type_row, type_col):
    offsets = []
    for off_row in range(-2 - type_row, 4 - type_row):
        for off_col in range(-2 - type_col, 4 - type_col):
            if max(abs(off_row), abs(off_col)) > 1:
                offsets.append((off_row, off_col))
    return offsets


SLOT_OF = {
    (e, f): {offset: s for s, offset in enumerate(slot_offsets(e, f))} for e in (0, 1) for f in (0, 1)
}


class Plan:
    def __init__(self, rows_dev, cols_dev, levels):
        self.rows_dev, self.cols_dev, self.levels = rows_dev, cols_dev, levels
        self.quads = rows_dev // 4
        self.pad = 2 if self.quads == 1 else 4
        self.window = 4 + 2 * self.pad
        self.grid = [(max(1, 2 * rows_dev >> l), max(1, 8 * cols_dev >> l)) for l in range(levels)]
        self.parents = [((r + 1) // 2, (c + 1) // 2) for r, c in self.grid]
        self.ne = [2 if r > 1 else 1 for r, _ in self.grid]
        self.offsets = [
            [(dr, dc) for dr, dc in AROUND if (pr > 1 or dr == 0) and (pc > 1 or dc == 0)]
            for pr, pc in self.parents
        ]
        self.top = max(l for l in range(levels) if self.offsets[l])
        self.far_levels = self.top + 1


def dot(a, b):
    return jnp.dot(a, b, preferred_element_type=F32)


def kernel(
    plan, probes, basis, up, down, coupling, ids, out,
    pbuf, s0, l1, l3, table, basis2, upv, downv, updup, downst, *rest,
):
    far_levels, top = plan.far_levels, plan.top
    weights, coup, rest = rest[:far_levels], rest[far_levels : 2 * far_levels], rest[2 * far_levels :]
    tops, rest = rest[: top - 2], rest[top - 2 :]
    local_sem, send_sem, precv, crecv, l1recv, l3recv = rest
    rows_dev, cols_dev, quads, pad = plan.rows_dev, plan.cols_dev, plan.quads, plan.pad
    g = lax.axis_index("gx")
    y = lax.axis_index("gy")
    quad, member = g // 4, g % 4
    quad_steps = (0,) if quads == 1 else (-1, 0, 1)

    def inside(row, col):
        return (row >= 0) & (row < rows_dev) & (col >= 0) & (col < cols_dev)

    near_partners = []
    for dq in quad_steps:
        for k in range(4):
            for dy in (-1, 0, 1):
                if (dq, k, dy) != (0, 0, 0):
                    near_partners.append((dq, k, dy))
    far_partners = [(kq, ky) for kq in range(quads) for ky in range(cols_dev) if (kq, ky) != (0, 0)]

    def near_device(dq, k, dy):
        return (quad + dq) * 4 + (member + k) % 4, y + dy

    def far_device(kq, ky):
        return (quad + kq) % quads * 4 + member, (y + ky) % cols_dev

    def met(row, col):
        return (abs(row // 4 - quad) <= 1) & (abs(col - y) <= 1)

    barrier = pltpu.get_barrier_semaphore()
    expected = jnp.int32(0)
    for partner in near_partners:
        row, col = near_device(*partner)
        valid = inside(row, col)

        @pl.when(valid)
        def _():
            pl.semaphore_signal(barrier, inc=1, device_id=(row, col), device_id_type=MESH)

        expected = expected + jnp.where(valid, 1, 0)
    for partner in far_partners:
        row, col = far_device(*partner)
        valid = jnp.logical_not(met(row, col))

        @pl.when(valid)
        def _():
            pl.semaphore_signal(barrier, inc=1, device_id=(row, col), device_id_type=MESH)

        expected = expected + jnp.where(valid, 1, 0)

    fetch = [
        pltpu.make_async_copy(probes, pbuf.at[1:3, 1:9], local_sem.at[0]),
        pltpu.make_async_copy(up.at[0:top], upv, local_sem.at[1]),
        pltpu.make_async_copy(down.at[0:top], downv, local_sem.at[2]),
    ]
    fetch_coup = [
        pltpu.make_async_copy(coupling.at[l], coup[l], local_sem.at[3 + l]) for l in range(far_levels)
    ]
    for copy in fetch + fetch_coup:
        copy.start()

    p_row_src = {0: slice(1, 3), 1: slice(2, 3), -1: slice(1, 2)}
    p_row_dst = {0: slice(1, 3), 1: slice(0, 1), -1: slice(3, 4)}
    p_col_src = {0: slice(1, 9), 1: slice(8, 9), -1: slice(1, 2)}
    p_col_dst = {0: slice(1, 9), 1: slice(0, 1), -1: slice(9, 10)}
    c_row_dst = {0: slice(1, 2), 1: slice(0, 1), -1: slice(2, 3)}
    c_col_src = {0: slice(1, 5), 1: slice(4, 5), -1: slice(1, 2)}
    c_col_dst = {0: slice(1, 5), 1: slice(0, 1), -1: slice(5, 6)}

    for du, dv in AROUND:

        @pl.when(jnp.logical_not(inside(g - du, y - dv)))
        def _():
            part = pbuf.at[p_row_dst[du], p_col_dst[dv]]
            part[...] = jnp.zeros(part.shape, BF16)
            part = s0.at[c_row_dst[du], c_col_dst[dv]]
            part[...] = jnp.zeros(part.shape, BF16)

    def clear(part):
        part[...] = jnp.zeros(part.shape, BF16)

    if quads == 1:
        clear(l1.at[0:pad])
        clear(l1.at[pad + 4 : 2 * pad + 4])
    else:

        @pl.when(quad == 0)
        def _():
            clear(l1.at[0:4])

        @pl.when(quad == quads - 1)
        def _():
            clear(l1.at[8:12])

    @pl.when(y == 0)
    def _():
        clear(l1.at[:, 0])

    @pl.when(y == cols_dev - 1)
    def _():
        clear(l1.at[:, 2])

    for level_top in tops:
        clear(level_top)

    basis_wide = basis[...]
    nothing = jnp.zeros((128, 64), BF16)
    basis2[0:128] = jnp.concatenate([basis_wide, nothing], axis=1)
    basis2[128:256] = jnp.concatenate([nothing, basis_wide], axis=1)

    fetch[1].wait()

    def make_updup(l):
        width = plan.ne[l] * 128
        wide = upv[l, 0 : 2 * plan.ne[l]].reshape(width, 64)
        updup[l, 0:width] = jnp.concatenate([wide, wide], axis=1)

    make_updup(0)
    fetch[0].wait()
    left_rows = jnp.concatenate(
        [
            jnp.concatenate([pbuf[1 + e, 1 + 2 * p], pbuf[1 + e, 2 + 2 * p]], axis=1)
            for e in (0, 1)
            for p in range(4)
        ],
        axis=0,
    )
    leaf = dot(left_rows, basis2[...]).astype(BF16)
    own = jnp.concatenate([leaf[0:128], leaf[128:256]], axis=1)
    s0[1, 1:5] = own.reshape(4, 32, 256)

    def halves(shape):
        return lax.broadcasted_iota(jnp.int32, shape, len(shape) - 1) // 64

    half32 = halves((32, 128))
    lifted = dot(own, updup[0, 0:256])
    own_row = pad + member
    for pc in (0, 1):
        first = lifted[64 * pc : 64 * pc + 32]
        second = lifted[64 * pc + 32 : 64 * pc + 64]
        l1[own_row, 1, pc] = jnp.where(half32 == 0, first, second).astype(BF16)

    pl.semaphore_wait(barrier, expected)

    sent = []

    def send(src, dst, recv, device, valid):
        copy = pltpu.make_async_remote_copy(
            src_ref=src, dst_ref=dst, send_sem=send_sem.at[len(sent)], recv_sem=recv,
            device_id=device, device_id_type=MESH,
        )
        sent.append((copy, valid))
        if valid is None:
            copy.start()
        else:
            pl.when(valid)(copy.start)

    def receive(dst, recv, valid):
        copy = pltpu.make_async_remote_copy(
            src_ref=dst, dst_ref=dst, send_sem=send_sem.at[0], recv_sem=recv,
            device_id=(g, y), device_id_type=MESH,
        )
        if valid is None:
            copy.wait_recv()
        else:
            pl.when(valid)(copy.wait_recv)

    ordered = sorted(near_partners, key=lambda t: (abs(t[2]), abs(t[0])))
    for dq, k, dy in ordered:
        device = near_device(dq, k, dy)
        row = pad - 4 * dq + member
        valid = None if (dq, dy) == (0, 0) else inside(*device)
        send(l1.at[own_row, 1], l1.at[row, 1 - dy], l1recv.at[row, 1 - dy], device, valid)
    for i, (du, dv) in sorted(enumerate(AROUND), key=lambda t: abs(t[1][1])):
        device = (g + du, y + dv)
        valid = inside(*device)
        send(s0.at[1:2, c_col_src[dv]], s0.at[c_row_dst[du], c_col_dst[dv]], crecv.at[i], device, valid)
        send(
            pbuf.at[p_row_src[du], p_col_src[dv]], pbuf.at[p_row_dst[du], p_col_dst[dv]],
            precv.at[i], device, valid,
        )

    for l in range(1, top):
        make_updup(l)

    def receive_l1(wanted):
        for dq, k, dy in ordered:
            if wanted(dq, dy):
                device = near_device(dq, k, dy)
                row = pad + 4 * dq + (member + k) % 4
                valid = None if (dq, dy) == (0, 0) else inside(*device)
                receive(l1.at[row, 1 + dy], l1recv.at[row, 1 + dy], valid)

    def level2(dq, side):
        parts = []
        for e in (0, 1):
            for pc in (0, 1):
                row = pad + 4 * dq + 2 * e
                parts.append(jnp.concatenate([l1[row, side, pc], l1[row + 1, side, pc]], axis=1))
        lift = dot(jnp.concatenate(parts, axis=0), updup[1, 0:256])
        both = [jnp.where(half32 == 0, lift[64 * e : 64 * e + 32], lift[64 * e + 32 : 64 * e + 64]) for e in (0, 1)]
        return jnp.concatenate(both, axis=1).astype(BF16)

    receive_l1(lambda dq, dy: dq == 0 and dy == 0)
    two = {(0, 0): level2(0, 1)}
    lift = dot(two[0, 0], updup[2, 0:256])
    l3[quad, y] = jnp.where(half32 == y % 2, lift, 0.0).astype(BF16)
    for kq, ky in far_partners:
        device = far_device(kq, ky)
        send(l3.at[quad, y], l3.at[quad, y], l3recv.at[quad, y], device, None)

    point_q = lax.broadcasted_iota(jnp.int32, (128, 128), 0)
    point_p = lax.broadcasted_iota(jnp.int32, (128, 128), 1)
    row_apart = (point_q // LEAF_COLS - point_p // LEAF_COLS).astype(F32)
    col_apart = (point_q % LEAF_COLS - point_p % LEAF_COLS).astype(F32)
    for i, (u, v) in enumerate([(u, v) for u in (-1, 0, 1) for v in (-1, 0, 1)]):
        dr = row_apart + float(u * LEAF_ROWS)
        dc = col_apart + float(v * LEAF_COLS)
        t = jnp.sqrt(3.0 * (dr * dr + dc * dc)) / LENGTH_SCALE
        table[128 * i : 128 * i + 128] = ((1.0 + t) * jnp.exp(-t)).astype(BF16)

    fetch[2].wait()
    for l in range(top):
        for e in range(plan.ne[l]):
            wide = jnp.concatenate([downv[l, 2 * e], downv[l, 2 * e + 1]], axis=1)
            for c in range(2 * plan.ne[l + 1]):
                downst[l, 64 * c : 64 * c + 64, 128 * e : 128 * e + 128] = wide

    empty = jnp.zeros((64, 64), BF16)
    for l in reversed(range(far_levels)):
        fetch_coup[l].wait()
        for i, (dr, dc) in enumerate(plan.offsets[l]):
            for se in range(plan.ne[l]):
                for sf in (0, 1):
                    for e in range(plan.ne[l]):
                        pair = []
                        for f in (0, 1):
                            slot = SLOT_OF[e, f].get((2 * dr + se - e, 2 * dc + sf - f))
                            pair.append(empty if slot is None else coup[l][ids[l, 2 * e + f, slot]])
                        c = 2 * se + sf
                        weights[l][i, 64 * c : 64 * c + 64, 128 * e : 128 * e + 128] = jnp.concatenate(pair, axis=1)

    receive_l1(lambda dq, dy: not (dq == 0 and dy == 0))
    pair_row = pad + 2 * (member // 2)
    far1 = jnp.zeros((64, 256), F32)
    for dr in (-1, 0, 1):
        row = pair_row + 2 * dr
        tiles = [
            jnp.concatenate([l1[row, side, pc], l1[row + 1, side, pc]], axis=1)
            for side, pc in ((0, 1), (1, 0), (1, 1), (2, 0))
        ]
        for dc in (-1, 0, 1):
            if (dr, dc) in plan.offsets[1]:
                lhs = jnp.concatenate([tiles[1 + dc], tiles[2 + dc]], axis=0)
                far1 = far1 + dot(lhs, weights[1][plan.offsets[1].index((dr, dc))])
    for dq in quad_steps:
        for dy in (-1, 0, 1):
            if (dq, dy) != (0, 0):
                two[dq, dy] = level2(dq, 1 + dy)
    far2 = jnp.zeros((32, 256), F32)
    for i, (dr, dc) in enumerate(plan.offsets[2]):
        far2 = far2 + dot(two[dr, dc], weights[2][i])

    for kq, ky in far_partners:
        row, col = (quad + kq) % quads, (y + ky) % cols_dev
        receive(l3.at[row, col], l3recv.at[row, col], None)
    for l in range(3, far_levels):
        pr_count, pc_count = plan.parents[l]
        level_top = tops[l - 3]
        if l == 3:
            for pr in range(pr_count):
                for pc in range(pc_count):
                    for e in range(plan.ne[3]):
                        level_top[1 + pr, 1 + pc, :, 128 * e : 128 * e + 128] = (
                            l3[2 * pr + e, 2 * pc] + l3[2 * pr + e, 2 * pc + 1]
                        )
        else:
            rows_below, cols_below = plan.grid[l]
            for r in range(rows_below):
                below = tops[l - 4][1 + r, 1 : 1 + cols_below].reshape(32 * cols_below, -1)
                lift = dot(below, updup[l - 1, 0 : below.shape[1]])
                for pc in range(pc_count):
                    first, second = lift[64 * pc : 64 * pc + 32], lift[64 * pc + 32 : 64 * pc + 64]
                    e = r % 2
                    level_top[1 + r // 2, 1 + pc, :, 128 * e : 128 * e + 128] = jnp.where(
                        half32 == 0, first, second
                    ).astype(BF16)

    def far_top(l):
        width = 128 * plan.ne[l]
        pr, pc = quad >> (l - 2), y >> (l - 2)
        total = jnp.zeros((32, width), F32)
        for i, (dr, dc) in enumerate(plan.offsets[l]):
            total = total + dot(tops[l - 3][1 + pr + dr, 1 + pc + dc], weights[l][i])
        return total

    local = None
    for l in reversed(range(3, far_levels)):
        total = far_top(l)
        if local is not None:
            total = total + dot(local, downst[l, 0 : local.shape[1], 0 : total.shape[1]])
        child = 2 * ((quad >> (l - 3)) % 2) + (y >> (l - 3)) % 2
        local = jnp.where(halves(total.shape) == child, total, 0.0).astype(BF16)
    total = far2 + dot(local, downst[2, 0 : local.shape[1], 0:256])
    lane = halves(total.shape)
    base = 2 * (g // 2 % 2)
    local = jnp.concatenate([jnp.where(lane == base + f, total, 0.0) for f in (0, 1)], axis=0).astype(BF16)
    total = far1 + dot(local, downst[1])
    base = 2 * (g % 2)
    local = jnp.concatenate(
        [jnp.where(lane == base + f, total[32 * pc : 32 * pc + 32], 0.0) for pc in (0, 1) for f in (0, 1)], axis=0
    ).astype(BF16)
    total = dot(local, downst[0])

    for i, (du, dv) in enumerate(AROUND):
        receive(s0.at[c_row_dst[du], c_col_dst[dv]], crecv.at[i], inside(g - du, y - dv))
    for i, (dr, dc) in enumerate(plan.offsets[0]):
        total = total + dot(s0[1 + dr, 1 + dc : 5 + dc].reshape(128, 256), weights[0][i])
    local = total.astype(BF16)
    local = jnp.concatenate([local[:, 0:128], local[:, 128:256]], axis=0)
    spread = lax.dot_general(local, basis2[...], (((1,), (1,)), ((), ())), preferred_element_type=F32)

    for i, (du, dv) in enumerate(AROUND):
        receive(pbuf.at[p_row_dst[du], p_col_dst[dv]], precv.at[i], inside(g - du, y - dv))
    for e in (0, 1):
        lhs = jnp.concatenate(
            [
                pbuf[1 + e + u, 1 + v : 9 + v].reshape(256, 128)
                for u in (-1, 0, 1)
                for v in (-1, 0, 1)
            ],
            axis=1,
        )
        near = dot(lhs, table[...])
        for b in range(8):
            p, f = b // 2, b % 2
            far = spread[128 * e + 32 * p : 128 * e + 32 * p + 32, 128 * f : 128 * f + 128]
            out[e, b] = (near[32 * b : 32 * b + 32] + far).astype(BF16)

    for copy, valid in sent:
        if valid is None:
            copy.wait_send()
        else:
            pl.when(valid)(copy.wait_send)


def shards(plan, probes, leaf_basis, up_transfer, down_transfer, coupling, far_ids):
    quads, cols_dev, far_levels, top = plan.quads, plan.cols_dev, plan.far_levels, plan.top
    dma = pltpu.SemaphoreType.DMA
    near_count = 3 * 4 * (1 if quads == 1 else 3) - 1
    send_count = near_count + 16 + quads * cols_dev - 1
    scratch = [
        pltpu.VMEM((4, 10, 32, 128), BF16),
        pltpu.VMEM((3, 6, 32, 256), BF16),
        pltpu.VMEM((plan.window, 3, 2, 32, 128), BF16),
        pltpu.VMEM((quads, cols_dev, 32, 128), BF16),
        pltpu.VMEM((9 * 128, 128), BF16),
        pltpu.VMEM((256, 128), BF16),
        pltpu.VMEM((top, 4, 64, 64), BF16),
        pltpu.VMEM((top, 4, 64, 64), BF16),
        pltpu.VMEM((top, 256, 128), BF16),
        pltpu.VMEM((top, 256, 256), BF16),
    ]
    for l in range(far_levels):
        scratch.append(pltpu.VMEM((len(plan.offsets[l]), 128 * plan.ne[l], 128 * plan.ne[l]), BF16))
    scratch += [pltpu.VMEM(coupling.shape[1:], BF16) for _ in range(far_levels)]
    for l in range(3, far_levels):
        pr, pc = plan.parents[l]
        scratch.append(pltpu.VMEM((pr + 2, pc + 2, 32, 128 * plan.ne[l]), BF16))
    scratch += [
        dma((3 + far_levels,)),
        dma((send_count,)),
        dma((8,)),
        dma((8,)),
        dma((plan.window, 3)),
        dma((quads, cols_dev)),
    ]
    anywhere = pl.BlockSpec(memory_space=pl.ANY)
    vmem = pl.BlockSpec(memory_space=pltpu.VMEM)
    return pl.pallas_call(
        functools.partial(kernel, plan),
        out_shape=jax.ShapeDtypeStruct(probes.shape, BF16),
        in_specs=[anywhere, vmem, anywhere, anywhere, anywhere, pl.BlockSpec(memory_space=pltpu.SMEM)],
        out_specs=vmem,
        scratch_shapes=scratch,
        compiler_params=pltpu.CompilerParams(
            collective_id=0, has_side_effects=True, vmem_limit_bytes=40 * 1024 * 1024
        ),
    )(probes, leaf_basis, up_transfer, down_transfer, coupling, far_ids)


def solution(mesh):
    in_specs = (P("gx", "gy", None, None), P(), P(), P(), P(), P())
    out_specs = P("gx", "gy", None, None)

    def run(probes, leaf_basis, up_transfer, down_transfer, coupling, far_ids):
        plan = Plan(mesh.shape["gx"], mesh.shape["gy"], coupling.shape[0])
        return jax.shard_map(
            functools.partial(shards, plan), mesh=mesh, in_specs=in_specs, out_specs=out_specs, check_vma=False
        )(probes, leaf_basis, up_transfer, down_transfer, coupling, far_ids)

    return run
```

```python
import functools

import jax
import jax.numpy as jnp
from jax import lax
from jax.experimental import pallas as pl
from jax.experimental.pallas import tpu as pltpu
from jax.sharding import PartitionSpec as P

LEAF_ROWS = 8
LEAF_COLS = 16
LENGTH_SCALE = 1.5
MESH = pl.DeviceIdType.MESH
BF16 = jnp.bfloat16
F32 = jnp.float32
AROUND = [(du, dv) for du in (-1, 0, 1) for dv in (-1, 0, 1) if (du, dv) != (0, 0)]


def slot_offsets(type_row, type_col):
    offsets = []
    for off_row in range(-2 - type_row, 4 - type_row):
        for off_col in range(-2 - type_col, 4 - type_col):
            if max(abs(off_row), abs(off_col)) > 1:
                offsets.append((off_row, off_col))
    return offsets


SLOT_OF = {
    (e, f): {offset: s for s, offset in enumerate(slot_offsets(e, f))} for e in (0, 1) for f in (0, 1)
}


class Plan:
    def __init__(self, rows_dev, cols_dev, levels):
        self.rows_dev, self.cols_dev, self.levels = rows_dev, cols_dev, levels
        self.quads = rows_dev // 4
        self.pad = 2 if self.quads == 1 else 4
        self.window = 4 + 2 * self.pad
        self.grid = [(max(1, 2 * rows_dev >> l), max(1, 8 * cols_dev >> l)) for l in range(levels)]
        self.parents = [((r + 1) // 2, (c + 1) // 2) for r, c in self.grid]
        self.ne = [2 if r > 1 else 1 for r, _ in self.grid]
        self.offsets = [
            [(dr, dc) for dr, dc in AROUND if (pr > 1 or dr == 0) and (pc > 1 or dc == 0)]
            for pr, pc in self.parents
        ]
        self.top = max(l for l in range(levels) if self.offsets[l])
        self.far_levels = self.top + 1


def dot(a, b):
    return jnp.dot(a, b, preferred_element_type=F32)


def kernel(
    plan, probes, basis, up, down, coupling, ids_hbm, out,
    pbuf, s0, l1, l3, table, basisv, ids, basis2, upv, downv, updup, downst, *rest,
):
    far_levels, top = plan.far_levels, plan.top
    weights, coup, rest = rest[:far_levels], rest[far_levels : 2 * far_levels], rest[2 * far_levels :]
    tops, rest = rest[: top - 2], rest[top - 2 :]
    local_sem, send_sem, precv, crecv, l1recv, l3recv = rest
    rows_dev, cols_dev, quads, pad = plan.rows_dev, plan.cols_dev, plan.quads, plan.pad
    g = lax.axis_index("gx")
    y = lax.axis_index("gy")
    quad, member = g // 4, g % 4
    quad_steps = (0,) if quads == 1 else (-1, 0, 1)

    def inside(row, col):
        return (row >= 0) & (row < rows_dev) & (col >= 0) & (col < cols_dev)

    near_partners = []
    for dq in quad_steps:
        for k in range(4):
            for dy in (-1, 0, 1):
                if (dq, k, dy) != (0, 0, 0):
                    near_partners.append((dq, k, dy))
    far_partners = [(kq, ky) for kq in range(quads) for ky in range(cols_dev) if (kq, ky) != (0, 0)]

    def near_device(dq, k, dy):
        return (quad + dq) * 4 + (member + k) % 4, y + dy

    def far_device(kq, ky):
        return (quad + kq) % quads * 4 + member, (y + ky) % cols_dev

    def met(row, col):
        return (abs(row // 4 - quad) <= 1) & (abs(col - y) <= 1)

    barrier = pltpu.get_barrier_semaphore()
    expected = jnp.int32(0)
    for partner in near_partners:
        row, col = near_device(*partner)
        valid = inside(row, col)

        @pl.when(valid)
        def _():
            pl.semaphore_signal(barrier, inc=1, device_id=(row, col), device_id_type=MESH)

        expected = expected + jnp.where(valid, 1, 0)
    for partner in far_partners:
        row, col = far_device(*partner)
        valid = jnp.logical_not(met(row, col))

        @pl.when(valid)
        def _():
            pl.semaphore_signal(barrier, inc=1, device_id=(row, col), device_id_type=MESH)

        expected = expected + jnp.where(valid, 1, 0)

    fetch = [
        pltpu.make_async_copy(probes, pbuf.at[1:3, 1:9], local_sem.at[0]),
        pltpu.make_async_copy(up.at[0:top], upv, local_sem.at[1]),
        pltpu.make_async_copy(down.at[0:top], downv, local_sem.at[2]),
        pltpu.make_async_copy(basis, basisv, local_sem.at[3]),
        pltpu.make_async_copy(ids_hbm, ids, local_sem.at[4]),
    ]
    fetch_coup = [
        pltpu.make_async_copy(coupling.at[l], coup[l], local_sem.at[5 + l]) for l in range(far_levels)
    ]
    for copy in fetch + fetch_coup:
        copy.start()

    p_row_src = {0: slice(1, 3), 1: slice(2, 3), -1: slice(1, 2)}
    p_row_dst = {0: slice(1, 3), 1: slice(0, 1), -1: slice(3, 4)}
    p_col_src = {0: slice(1, 9), 1: slice(8, 9), -1: slice(1, 2)}
    p_col_dst = {0: slice(1, 9), 1: slice(0, 1), -1: slice(9, 10)}
    c_row_dst = {0: slice(1, 2), 1: slice(0, 1), -1: slice(2, 3)}
    c_col_src = {0: slice(1, 5), 1: slice(4, 5), -1: slice(1, 2)}
    c_col_dst = {0: slice(1, 5), 1: slice(0, 1), -1: slice(5, 6)}

    for du, dv in AROUND:

        @pl.when(jnp.logical_not(inside(g - du, y - dv)))
        def _():
            part = pbuf.at[p_row_dst[du], p_col_dst[dv]]
            part[...] = jnp.zeros(part.shape, BF16)
            part = s0.at[c_row_dst[du], c_col_dst[dv]]
            part[...] = jnp.zeros(part.shape, BF16)

    def clear(part):
        part[...] = jnp.zeros(part.shape, BF16)

    if quads == 1:
        clear(l1.at[0:pad])
        clear(l1.at[pad + 4 : 2 * pad + 4])
    else:

        @pl.when(quad == 0)
        def _():
            clear(l1.at[0:4])

        @pl.when(quad == quads - 1)
        def _():
            clear(l1.at[8:12])

    @pl.when(y == 0)
    def _():
        clear(l1.at[:, 0])

    @pl.when(y == cols_dev - 1)
    def _():
        clear(l1.at[:, 2])

    for level_top in tops:
        clear(level_top)

    basis2[...] = jnp.zeros((128, 256), BF16)
    fetch[3].wait()
    basis2[0:64, 0:128] = basisv[...]
    basis2[64:128, 128:256] = basisv[...]

    fetch[1].wait()

    def make_updup(l):
        width = plan.ne[l] * 128
        wide = upv[l, 0 : 2 * plan.ne[l]].reshape(width, 64)
        updup[l, 0:width] = jnp.concatenate([wide, wide], axis=1)

    make_updup(0)
    fetch[0].wait()
    left_rows = jnp.concatenate(
        [
            jnp.concatenate([pbuf[1 + e, 1 + 2 * p], pbuf[1 + e, 2 + 2 * p]], axis=1)
            for e in (0, 1)
            for p in range(4)
        ],
        axis=0,
    )
    leaf = lax.dot_general(
        left_rows, basis2[...], (((1,), (1,)), ((), ())), preferred_element_type=F32
    ).astype(BF16)
    own = jnp.concatenate([leaf[0:128], leaf[128:256]], axis=1)
    s0[1, 1:5] = own.reshape(4, 32, 256)

    def halves(shape):
        return lax.broadcasted_iota(jnp.int32, shape, len(shape) - 1) // 64

    half32 = halves((32, 128))
    lifted = dot(own, updup[0, 0:256])
    own_row = pad + member
    for pc in (0, 1):
        first = lifted[64 * pc : 64 * pc + 32]
        second = lifted[64 * pc + 32 : 64 * pc + 64]
        l1[own_row, 1, pc] = jnp.where(half32 == 0, first, second).astype(BF16)

    pl.semaphore_wait(barrier, expected)

    sent = []

    def send(src, dst, recv, device, valid):
        copy = pltpu.make_async_remote_copy(
            src_ref=src, dst_ref=dst, send_sem=send_sem.at[len(sent)], recv_sem=recv,
            device_id=device, device_id_type=MESH,
        )
        sent.append((copy, valid))
        if valid is None:
            copy.start()
        else:
            pl.when(valid)(copy.start)

    def receive(dst, recv, valid):
        copy = pltpu.make_async_remote_copy(
            src_ref=dst, dst_ref=dst, send_sem=send_sem.at[0], recv_sem=recv,
            device_id=(g, y), device_id_type=MESH,
        )
        if valid is None:
            copy.wait_recv()
        else:
            pl.when(valid)(copy.wait_recv)

    ordered = sorted(near_partners, key=lambda t: (abs(t[2]), abs(t[0])))
    for dq, k, dy in ordered:
        device = near_device(dq, k, dy)
        row = pad - 4 * dq + member
        valid = None if (dq, dy) == (0, 0) else inside(*device)
        send(l1.at[own_row, 1], l1.at[row, 1 - dy], l1recv.at[row, 1 - dy], device, valid)
    for i, (du, dv) in sorted(enumerate(AROUND), key=lambda t: abs(t[1][1])):
        device = (g + du, y + dv)
        valid = inside(*device)
        send(s0.at[1:2, c_col_src[dv]], s0.at[c_row_dst[du], c_col_dst[dv]], crecv.at[i], device, valid)
        send(
            pbuf.at[p_row_src[du], p_col_src[dv]], pbuf.at[p_row_dst[du], p_col_dst[dv]],
            precv.at[i], device, valid,
        )

    for l in range(1, top):
        make_updup(l)

    def receive_l1(wanted):
        for dq, k, dy in ordered:
            if wanted(dq, dy):
                device = near_device(dq, k, dy)
                row = pad + 4 * dq + (member + k) % 4
                valid = None if (dq, dy) == (0, 0) else inside(*device)
                receive(l1.at[row, 1 + dy], l1recv.at[row, 1 + dy], valid)

    def level2(dq, side):
        parts = []
        for e in (0, 1):
            for pc in (0, 1):
                row = pad + 4 * dq + 2 * e
                parts.append(jnp.concatenate([l1[row, side, pc], l1[row + 1, side, pc]], axis=1))
        lift = dot(jnp.concatenate(parts, axis=0), updup[1, 0:256])
        both = [jnp.where(half32 == 0, lift[64 * e : 64 * e + 32], lift[64 * e + 32 : 64 * e + 64]) for e in (0, 1)]
        return jnp.concatenate(both, axis=1).astype(BF16)

    receive_l1(lambda dq, dy: dq == 0 and dy == 0)
    two = {(0, 0): level2(0, 1)}
    lift = dot(two[0, 0], updup[2, 0:256])
    l3[quad, y] = jnp.where(half32 == y % 2, lift, 0.0).astype(BF16)
    for kq, ky in far_partners:
        device = far_device(kq, ky)
        send(l3.at[quad, y], l3.at[quad, y], l3recv.at[quad, y], device, None)

    point_q = lax.broadcasted_iota(jnp.int32, (128, 128), 0)
    point_p = lax.broadcasted_iota(jnp.int32, (128, 128), 1)
    row_apart = (point_q // LEAF_COLS - point_p // LEAF_COLS).astype(F32)
    col_apart = (point_q % LEAF_COLS - point_p % LEAF_COLS).astype(F32)
    for i, (u, v) in enumerate([(u, v) for u in (-1, 0, 1) for v in (-1, 0, 1)]):
        dr = row_apart + float(u * LEAF_ROWS)
        dc = col_apart + float(v * LEAF_COLS)
        t = jnp.sqrt(3.0 * (dr * dr + dc * dc)) / LENGTH_SCALE
        table[128 * i : 128 * i + 128] = ((1.0 + t) * jnp.exp(-t)).astype(BF16)

    fetch[2].wait()
    for l in range(top):
        for e in range(plan.ne[l]):
            wide = jnp.concatenate([downv[l, 2 * e], downv[l, 2 * e + 1]], axis=1)
            for c in range(2 * plan.ne[l + 1]):
                downst[l, 64 * c : 64 * c + 64, 128 * e : 128 * e + 128] = wide

    empty = jnp.zeros((64, 64), BF16)
    fetch[4].wait()
    for l in reversed(range(far_levels)):
        fetch_coup[l].wait()
        for i, (dr, dc) in enumerate(plan.offsets[l]):
            for se in range(plan.ne[l]):
                for sf in (0, 1):
                    for e in range(plan.ne[l]):
                        pair = []
                        for f in (0, 1):
                            slot = SLOT_OF[e, f].get((2 * dr + se - e, 2 * dc + sf - f))
                            pair.append(empty if slot is None else coup[l][ids[l, 2 * e + f, slot]])
                        c = 2 * se + sf
                        weights[l][i, 64 * c : 64 * c + 64, 128 * e : 128 * e + 128] = jnp.concatenate(pair, axis=1)

    receive_l1(lambda dq, dy: not (dq == 0 and dy == 0))
    pair_row = pad + 2 * (member // 2)
    far1 = jnp.zeros((64, 256), F32)
    for dr in (-1, 0, 1):
        row = pair_row + 2 * dr
        tiles = [
            jnp.concatenate([l1[row, side, pc], l1[row + 1, side, pc]], axis=1)
            for side, pc in ((0, 1), (1, 0), (1, 1), (2, 0))
        ]
        for dc in (-1, 0, 1):
            if (dr, dc) in plan.offsets[1]:
                lhs = jnp.concatenate([tiles[1 + dc], tiles[2 + dc]], axis=0)
                far1 = far1 + dot(lhs, weights[1][plan.offsets[1].index((dr, dc))])
    for dq in quad_steps:
        for dy in (-1, 0, 1):
            if (dq, dy) != (0, 0):
                two[dq, dy] = level2(dq, 1 + dy)
    far2 = jnp.zeros((32, 256), F32)
    for i, (dr, dc) in enumerate(plan.offsets[2]):
        far2 = far2 + dot(two[dr, dc], weights[2][i])

    for kq, ky in far_partners:
        row, col = (quad + kq) % quads, (y + ky) % cols_dev
        receive(l3.at[row, col], l3recv.at[row, col], None)
    for l in range(3, far_levels):
        pr_count, pc_count = plan.parents[l]
        level_top = tops[l - 3]
        if l == 3:
            for pr in range(pr_count):
                for pc in range(pc_count):
                    for e in range(plan.ne[3]):
                        level_top[1 + pr, 1 + pc, :, 128 * e : 128 * e + 128] = (
                            l3[2 * pr + e, 2 * pc] + l3[2 * pr + e, 2 * pc + 1]
                        )
        else:
            rows_below, cols_below = plan.grid[l]
            for r in range(rows_below):
                below = tops[l - 4][1 + r, 1 : 1 + cols_below].reshape(32 * cols_below, -1)
                lift = dot(below, updup[l - 1, 0 : below.shape[1]])
                for pc in range(pc_count):
                    first, second = lift[64 * pc : 64 * pc + 32], lift[64 * pc + 32 : 64 * pc + 64]
                    e = r % 2
                    level_top[1 + r // 2, 1 + pc, :, 128 * e : 128 * e + 128] = jnp.where(
                        half32 == 0, first, second
                    ).astype(BF16)

    def far_top(l):
        width = 128 * plan.ne[l]
        pr, pc = quad >> (l - 2), y >> (l - 2)
        total = jnp.zeros((32, width), F32)
        for i, (dr, dc) in enumerate(plan.offsets[l]):
            total = total + dot(tops[l - 3][1 + pr + dr, 1 + pc + dc], weights[l][i])
        return total

    local = None
    for l in reversed(range(3, far_levels)):
        total = far_top(l)
        if local is not None:
            total = total + dot(local, downst[l, 0 : local.shape[1], 0 : total.shape[1]])
        child = 2 * ((quad >> (l - 3)) % 2) + (y >> (l - 3)) % 2
        local = jnp.where(halves(total.shape) == child, total, 0.0).astype(BF16)
    total = far2 + dot(local, downst[2, 0 : local.shape[1], 0:256])
    lane = halves(total.shape)
    base = 2 * (g // 2 % 2)
    local = jnp.concatenate([jnp.where(lane == base + f, total, 0.0) for f in (0, 1)], axis=0).astype(BF16)
    total = far1 + dot(local, downst[1])
    base = 2 * (g % 2)
    local = jnp.concatenate(
        [jnp.where(lane == base + f, total[32 * pc : 32 * pc + 32], 0.0) for pc in (0, 1) for f in (0, 1)], axis=0
    ).astype(BF16)
    total = dot(local, downst[0])

    for i, (du, dv) in enumerate(AROUND):
        receive(s0.at[c_row_dst[du], c_col_dst[dv]], crecv.at[i], inside(g - du, y - dv))
    for i, (dr, dc) in enumerate(plan.offsets[0]):
        total = total + dot(s0[1 + dr, 1 + dc : 5 + dc].reshape(128, 256), weights[0][i])
    local = total.astype(BF16)
    local = jnp.concatenate([local[:, 0:128], local[:, 128:256]], axis=0)
    spread = dot(local, basis2[...])

    for i, (du, dv) in enumerate(AROUND):
        receive(pbuf.at[p_row_dst[du], p_col_dst[dv]], precv.at[i], inside(g - du, y - dv))
    for e in (0, 1):
        lhs = jnp.concatenate(
            [
                pbuf[1 + e + u, 1 + v : 9 + v].reshape(256, 128)
                for u in (-1, 0, 1)
                for v in (-1, 0, 1)
            ],
            axis=1,
        )
        near = dot(lhs, table[...])
        for b in range(8):
            p, f = b // 2, b % 2
            far = spread[128 * e + 32 * p : 128 * e + 32 * p + 32, 128 * f : 128 * f + 128]
            out[e, b] = (near[32 * b : 32 * b + 32] + far).astype(BF16)

    for copy, valid in sent:
        if valid is None:
            copy.wait_send()
        else:
            pl.when(valid)(copy.wait_send)


def shards(plan, probes, leaf_basis, up_transfer, down_transfer, coupling, far_ids):
    quads, cols_dev, far_levels, top = plan.quads, plan.cols_dev, plan.far_levels, plan.top
    dma = pltpu.SemaphoreType.DMA
    near_count = 3 * 4 * (1 if quads == 1 else 3) - 1
    send_count = near_count + 16 + quads * cols_dev - 1
    scratch = [
        pltpu.VMEM((4, 10, 32, 128), BF16),
        pltpu.VMEM((3, 6, 32, 256), BF16),
        pltpu.VMEM((plan.window, 3, 2, 32, 128), BF16),
        pltpu.VMEM((quads, cols_dev, 32, 128), BF16),
        pltpu.VMEM((9 * 128, 128), BF16),
        pltpu.VMEM((64, 128), BF16),
        pltpu.SMEM(far_ids.shape, jnp.int32),
        pltpu.VMEM((128, 256), BF16),
        pltpu.VMEM((top, 4, 64, 64), BF16),
        pltpu.VMEM((top, 4, 64, 64), BF16),
        pltpu.VMEM((top, 256, 128), BF16),
        pltpu.VMEM((top, 256, 256), BF16),
    ]
    for l in range(far_levels):
        scratch.append(pltpu.VMEM((len(plan.offsets[l]), 128 * plan.ne[l], 128 * plan.ne[l]), BF16))
    scratch += [pltpu.VMEM(coupling.shape[1:], BF16) for _ in range(far_levels)]
    for l in range(3, far_levels):
        pr, pc = plan.parents[l]
        scratch.append(pltpu.VMEM((pr + 2, pc + 2, 32, 128 * plan.ne[l]), BF16))
    scratch += [
        dma((5 + far_levels,)),
        dma((send_count,)),
        dma((8,)),
        dma((8,)),
        dma((plan.window, 3)),
        dma((quads, cols_dev)),
    ]
    anywhere = pl.BlockSpec(memory_space=pltpu.HBM)
    vmem = pl.BlockSpec(memory_space=pltpu.VMEM)
    return pl.pallas_call(
        functools.partial(kernel, plan),
        out_shape=jax.ShapeDtypeStruct(probes.shape, BF16),
        in_specs=[anywhere] * 6,
        out_specs=vmem,
        scratch_shapes=scratch,
        compiler_params=pltpu.CompilerParams(
            collective_id=0, has_side_effects=True, vmem_limit_bytes=60 * 1024 * 1024
        ),
    )(probes, leaf_basis.T, up_transfer, down_transfer, coupling, far_ids)


def solution(mesh):
    in_specs = (P("gx", "gy", None, None), P(), P(), P(), P(), P())
    out_specs = P("gx", "gy", None, None)

    def run(probes, leaf_basis, up_transfer, down_transfer, coupling, far_ids):
        plan = Plan(mesh.shape["gx"], mesh.shape["gy"], coupling.shape[0])
        return jax.shard_map(
            functools.partial(shards, plan), mesh=mesh, in_specs=in_specs, out_specs=out_specs, check_vma=False
        )(probes, leaf_basis, up_transfer, down_transfer, coupling, far_ids)

    return run
```

```python
import functools

import jax
import jax.numpy as jnp
from jax import lax
from jax.experimental import pallas as pl
from jax.experimental.pallas import tpu as pltpu
from jax.sharding import PartitionSpec as P

LEAF_ROWS = 8
LEAF_COLS = 16
LENGTH_SCALE = 1.5
MESH = pl.DeviceIdType.MESH
BF16 = jnp.bfloat16
F32 = jnp.float32
AROUND = [(du, dv) for du in (-1, 0, 1) for dv in (-1, 0, 1) if (du, dv) != (0, 0)]


def slot_offsets(type_row, type_col):
    offsets = []
    for off_row in range(-2 - type_row, 4 - type_row):
        for off_col in range(-2 - type_col, 4 - type_col):
            if max(abs(off_row), abs(off_col)) > 1:
                offsets.append((off_row, off_col))
    return offsets


SLOT_OF = {
    (e, f): {offset: s for s, offset in enumerate(slot_offsets(e, f))} for e in (0, 1) for f in (0, 1)
}


class Plan:
    def __init__(self, rows_dev, cols_dev, levels):
        self.rows_dev, self.cols_dev, self.levels = rows_dev, cols_dev, levels
        self.quads = rows_dev // 4
        self.pad = 2 if self.quads == 1 else 4
        self.window = 4 + 2 * self.pad
        self.grid = [(max(1, 2 * rows_dev >> l), max(1, 8 * cols_dev >> l)) for l in range(levels)]
        self.parents = [((r + 1) // 2, (c + 1) // 2) for r, c in self.grid]
        self.ne = [2 if r > 1 else 1 for r, _ in self.grid]
        self.offsets = [
            [(dr, dc) for dr, dc in AROUND if (pr > 1 or dr == 0) and (pc > 1 or dc == 0)]
            for pr, pc in self.parents
        ]
        self.top = max(l for l in range(levels) if self.offsets[l])
        self.far_levels = self.top + 1


def dot(a, b):
    return jnp.dot(a, b, preferred_element_type=F32)


def kernel(
    plan, probes, basis, up, down, coupling, ids_hbm, out,
    pbuf, s0, l1, l1side, s2, l3, table, basisv, ids, basis2, upv, downv, updup, downst, *rest,
):
    far_levels, top = plan.far_levels, plan.top
    weights, coup, rest = rest[:far_levels], rest[far_levels : 2 * far_levels], rest[2 * far_levels :]
    tops, rest = rest[: top - 2], rest[top - 2 :]
    local_sem, send_sem, rowrecv, colrecv, cornerrecv, l1recv, siderecv, l3recv = rest
    rows_dev, cols_dev, quads, pad = plan.rows_dev, plan.cols_dev, plan.quads, plan.pad
    g = lax.axis_index("gx")
    y = lax.axis_index("gy")
    quad, member = g // 4, g % 4
    quad_steps = (0,) if quads == 1 else (-1, 0, 1)

    def inside(row, col):
        return (row >= 0) & (row < rows_dev) & (col >= 0) & (col < cols_dev)

    near_partners = [(dq, k) for dq in quad_steps for k in range(4) if (dq, k) != (0, 0)]
    far_partners = [(kq, ky) for kq in range(quads) for ky in range(cols_dev) if (kq, ky) != (0, 0)]

    def near_device(dq, k):
        return (quad + dq) * 4 + (member + k) % 4, y

    def far_device(kq, ky):
        return (quad + kq) % quads * 4 + member, (y + ky) % cols_dev

    def met(row, col):
        return (abs(row // 4 - quad) <= 1) & (col == y)

    barrier = pltpu.get_barrier_semaphore()
    expected = jnp.int32(0)
    for partner in near_partners:
        row, col = near_device(*partner)
        valid = inside(row, col)

        @pl.when(valid)
        def _():
            pl.semaphore_signal(barrier, inc=1, device_id=(row, col), device_id_type=MESH)

        expected = expected + jnp.where(valid, 1, 0)
    for partner in far_partners:
        row, col = far_device(*partner)
        valid = jnp.logical_not(met(row, col))

        @pl.when(valid)
        def _():
            pl.semaphore_signal(barrier, inc=1, device_id=(row, col), device_id_type=MESH)

        expected = expected + jnp.where(valid, 1, 0)

    fetch = [
        pltpu.make_async_copy(probes, pbuf.at[1:3, 1:9], local_sem.at[0]),
        pltpu.make_async_copy(up.at[0:top], upv, local_sem.at[1]),
        pltpu.make_async_copy(down.at[0:top], downv, local_sem.at[2]),
        pltpu.make_async_copy(basis, basisv, local_sem.at[3]),
        pltpu.make_async_copy(ids_hbm, ids, local_sem.at[4]),
    ]
    fetch_coup = [
        pltpu.make_async_copy(coupling.at[l], coup[l], local_sem.at[5 + l]) for l in range(far_levels)
    ]
    for copy in fetch + fetch_coup:
        copy.start()

    def clear(part):
        part[...] = jnp.zeros(part.shape, BF16)

    halo_row = {1: 0, -1: 2}
    probe_row = {1: 0, -1: 3}
    own_adjacent = {1: 2, -1: 1}
    far_half = {1: slice(0, 128), -1: slice(128, 256)}
    near_half = {1: slice(128, 256), -1: slice(0, 128)}
    probe_side = {1: slice(0, 1), -1: slice(9, 10)}
    coef_side = {1: slice(0, 1), -1: slice(5, 6)}
    own_probe_edge = {1: slice(8, 9), -1: slice(1, 2)}
    own_coef_edge = {1: slice(4, 5), -1: slice(1, 2)}
    side_of = {1: 0, -1: 1}
    signs = (1, -1)

    def row_inside(row):
        return (row >= 0) & (row < rows_dev)

    def col_inside(col):
        return (col >= 0) & (col < cols_dev)

    for d in signs:

        @pl.when(jnp.logical_not(row_inside(g - d)))
        def _():
            clear(pbuf.at[probe_row[d]])
            clear(s0.at[halo_row[d]])

        @pl.when(jnp.logical_not(col_inside(y - d)))
        def _():
            clear(pbuf.at[:, probe_side[d]])
            clear(s0.at[:, coef_side[d]])
            clear(l1side.at[:, side_of[d]])
            clear(s2.at[:, 1 - d])

    if quads == 1:
        for part in (l1, l1side):
            clear(part.at[0:pad])
            clear(part.at[pad + 4 : 2 * pad + 4])
    else:

        @pl.when(quad == 0)
        def _():
            clear(l1.at[0:4])

        @pl.when(quad == quads - 1)
        def _():
            clear(l1.at[8:12])

    for level_top in tops:
        clear(level_top)

    basis2[...] = jnp.zeros((128, 256), BF16)
    fetch[3].wait()
    basis2[0:64, 0:128] = basisv[...]
    basis2[64:128, 128:256] = basisv[...]

    fetch[1].wait()

    def make_updup(l):
        width = plan.ne[l] * 128
        wide = upv[l, 0 : 2 * plan.ne[l]].reshape(width, 64)
        updup[l, 0:width] = jnp.concatenate([wide, wide], axis=1)

    make_updup(0)
    fetch[0].wait()
    left_rows = jnp.concatenate(
        [
            jnp.concatenate([pbuf[1 + e, 1 + 2 * p], pbuf[1 + e, 2 + 2 * p]], axis=1)
            for e in (0, 1)
            for p in range(4)
        ],
        axis=0,
    )
    leaf = lax.dot_general(
        left_rows, basis2[...], (((1,), (1,)), ((), ())), preferred_element_type=F32
    ).astype(BF16)
    own = jnp.concatenate([leaf[0:128], leaf[128:256]], axis=1)
    s0[1, 1:5] = own.reshape(4, 32, 256)

    def halves(shape):
        return lax.broadcasted_iota(jnp.int32, shape, len(shape) - 1) // 64

    half32 = halves((32, 128))
    lifted = dot(own, updup[0, 0:256])
    own_row = pad + member
    for pc in (0, 1):
        first = lifted[64 * pc : 64 * pc + 32]
        second = lifted[64 * pc + 32 : 64 * pc + 64]
        l1[own_row, pc] = jnp.where(half32 == 0, first, second).astype(BF16)

    pl.semaphore_wait(barrier, expected)

    sent = []

    def send(src, dst, recv, device, valid):
        copy = pltpu.make_async_remote_copy(
            src_ref=src, dst_ref=dst, send_sem=send_sem.at[len(sent)], recv_sem=recv,
            device_id=device, device_id_type=MESH,
        )
        sent.append((copy, valid))
        if valid is None:
            copy.start()
        else:
            pl.when(valid)(copy.start)

    def receive(dst, recv, valid):
        copy = pltpu.make_async_remote_copy(
            src_ref=dst, dst_ref=dst, send_sem=send_sem.at[0], recv_sem=recv,
            device_id=(g, y), device_id_type=MESH,
        )
        if valid is None:
            copy.wait_recv()
        else:
            pl.when(valid)(copy.wait_recv)

    ordered = sorted(near_partners, key=lambda t: abs(t[0]))
    for dq, k in ordered:
        device = near_device(dq, k)
        row = pad - 4 * dq + member
        valid = None if dq == 0 else inside(*device)
        send(l1.at[own_row], l1.at[row], l1recv.at[row], device, valid)

    pieces = [(slice(1, 3), slice(1, 2)), (slice(7, 9), slice(4, 5)), (slice(3, 7), slice(2, 4))]

    def send_rows(piece):
        probe_cols, coef_cols = pieces[piece]
        for d in signs:
            device, valid = (g + d, y), row_inside(g + d)
            send(
                s0.at[1, coef_cols, :, far_half[d]], s0.at[halo_row[d], coef_cols, :, far_half[d]],
                rowrecv.at[piece, side_of[d], 0], device, valid,
            )
            send(
                pbuf.at[own_adjacent[d], probe_cols], pbuf.at[probe_row[d], probe_cols],
                rowrecv.at[piece, side_of[d], 1], device, valid,
            )

    def receive_rows(piece):
        probe_cols, coef_cols = pieces[piece]
        for d in signs:
            valid = row_inside(g - d)
            receive(s0.at[halo_row[d], coef_cols, :, far_half[d]], rowrecv.at[piece, side_of[d], 0], valid)
            receive(pbuf.at[probe_row[d], probe_cols], rowrecv.at[piece, side_of[d], 1], valid)

    send_rows(0)
    send_rows(1)
    for d in signs:
        device, valid = (g, y + d), col_inside(y + d)
        send(s0.at[1, own_coef_edge[d]], s0.at[1, coef_side[d]], colrecv.at[side_of[d], 0], device, valid)
        send(
            pbuf.at[1:3, own_probe_edge[d]], pbuf.at[1:3, probe_side[d]], colrecv.at[side_of[d], 1], device, valid
        )
    send_rows(2)

    for l in range(1, top):
        make_updup(l)

    point_q = lax.broadcasted_iota(jnp.int32, (128, 128), 0)
    point_p = lax.broadcasted_iota(jnp.int32, (128, 128), 1)
    row_apart = (point_q // LEAF_COLS - point_p // LEAF_COLS).astype(F32)
    col_apart = (point_q % LEAF_COLS - point_p % LEAF_COLS).astype(F32)
    for i, (u, v) in enumerate([(u, v) for u in (-1, 0, 1) for v in (-1, 0, 1)]):
        dr = row_apart + float(u * LEAF_ROWS)
        dc = col_apart + float(v * LEAF_COLS)
        t = jnp.sqrt(3.0 * (dr * dr + dc * dc)) / LENGTH_SCALE
        table[128 * i : 128 * i + 128] = ((1.0 + t) * jnp.exp(-t)).astype(BF16)

    for dq, k in ordered:
        row = pad + 4 * dq + (member + k) % 4
        receive(l1.at[row], l1recv.at[row], None if dq == 0 else inside(*near_device(dq, k)))
    parts = []
    for dq in quad_steps:
        for e in (0, 1):
            for pc in (0, 1):
                row = pad + 4 * dq + 2 * e
                parts.append(jnp.concatenate([l1[row, pc], l1[row + 1, pc]], axis=1))
    lift = dot(jnp.concatenate(parts, axis=0), updup[1, 0:256])
    for i, dq in enumerate(quad_steps):
        both = []
        for e in (0, 1):
            at = 128 * i + 64 * e
            both.append(jnp.where(half32 == 0, lift[at : at + 32], lift[at + 32 : at + 64]))
        s2[i, 1] = jnp.concatenate(both, axis=1).astype(BF16)
    lift = dot(s2[quad_steps.index(0), 1], updup[2, 0:256])
    l3[quad, y] = jnp.where(half32 == y % 2, lift, 0.0).astype(BF16)
    for kq, ky in far_partners:
        device = far_device(kq, ky)
        send(l3.at[quad, y], l3.at[quad, y], l3recv.at[quad, y], device, None)
    rows_sent = slice(pad, pad + 4) if quads == 1 else slice(0, plan.window)
    for d in signs:
        device, valid = (g, y + d), col_inside(y + d)
        send(l1.at[rows_sent, (1 + d) // 2], l1side.at[rows_sent, side_of[d]], siderecv.at[side_of[d], 0], device, valid)
        send(s2.at[:, 1], s2.at[:, 1 - d], siderecv.at[side_of[d], 1], device, valid)

    def adjacent(parents):
        rows = [
            jnp.concatenate([pbuf[probe_row[d], 2 * p - 1], pbuf[probe_row[d], 2 * p]], axis=1)
            for d in signs
            for p in parents
        ]
        coefs = lax.dot_general(
            jnp.concatenate(rows, axis=0), basis2[...], (((1,), (1,)), ((), ())), preferred_element_type=F32
        ).astype(BF16)
        at = 0
        for d in signs:
            for p in parents:
                s0[halo_row[d], p, :, near_half[d]] = coefs[at : at + 32]
                at += 32

    receive_rows(0)
    receive_rows(1)
    adjacent((1, 4))
    for d in signs:
        for v in signs:
            device, valid = (g, y + v), row_inside(g - d) & col_inside(y + v)
            send(
                s0.at[halo_row[d], own_coef_edge[v]], s0.at[halo_row[d], coef_side[v]],
                cornerrecv.at[side_of[d], side_of[v], 0], device, valid,
            )
            send(
                pbuf.at[probe_row[d], own_probe_edge[v]], pbuf.at[probe_row[d], probe_side[v]],
                cornerrecv.at[side_of[d], side_of[v], 1], device, valid,
            )

    fetch[2].wait()
    for l in range(top):
        for e in range(plan.ne[l]):
            wide = jnp.concatenate([downv[l, 2 * e], downv[l, 2 * e + 1]], axis=1)
            for c in range(2 * plan.ne[l + 1]):
                downst[l, 64 * c : 64 * c + 64, 128 * e : 128 * e + 128] = wide

    empty = jnp.zeros((64, 64), BF16)
    fetch[4].wait()
    for l in reversed(range(far_levels)):
        fetch_coup[l].wait()
        for i, (dr, dc) in enumerate(plan.offsets[l]):
            for se in range(plan.ne[l]):
                for sf in (0, 1):
                    for e in range(plan.ne[l]):
                        pair = []
                        for f in (0, 1):
                            slot = SLOT_OF[e, f].get((2 * dr + se - e, 2 * dc + sf - f))
                            pair.append(empty if slot is None else coup[l][ids[l, 2 * e + f, slot]])
                        c = 2 * se + sf
                        weights[l][i, 64 * c : 64 * c + 64, 128 * e : 128 * e + 128] = jnp.concatenate(pair, axis=1)

    for d in signs:
        valid = col_inside(y - d)
        receive(l1side.at[rows_sent, side_of[d]], siderecv.at[side_of[d], 0], valid)
        receive(s2.at[:, 1 - d], siderecv.at[side_of[d], 1], valid)
        receive(s0.at[1, coef_side[d]], colrecv.at[side_of[d], 0], valid)
        receive(pbuf.at[1:3, probe_side[d]], colrecv.at[side_of[d], 1], valid)
    for kq, ky in far_partners:
        row, col = (quad + kq) % quads, (y + ky) % cols_dev
        receive(l3.at[row, col], l3recv.at[row, col], None)
    receive_rows(2)
    for d in signs:
        for v in signs:
            valid = row_inside(g - d) & col_inside(y - v)
            receive(s0.at[halo_row[d], coef_side[v]], cornerrecv.at[side_of[d], side_of[v], 0], valid)
            receive(pbuf.at[probe_row[d], probe_side[v]], cornerrecv.at[side_of[d], side_of[v], 1], valid)
    adjacent((2, 3))

    pair_row = pad + 2 * (member // 2)
    far1 = jnp.zeros((64, 256), F32)
    for dr in (-1, 0, 1):
        row = pair_row + 2 * dr
        tiles = [
            jnp.concatenate([ref[row, at], ref[row + 1, at]], axis=1)
            for ref, at in ((l1side, 0), (l1, 0), (l1, 1), (l1side, 1))
        ]
        for dc in (-1, 0, 1):
            if (dr, dc) in plan.offsets[1]:
                lhs = jnp.concatenate([tiles[1 + dc], tiles[2 + dc]], axis=0)
                far1 = far1 + dot(lhs, weights[1][plan.offsets[1].index((dr, dc))])
    far2 = jnp.zeros((32, 256), F32)
    for i, (dr, dc) in enumerate(plan.offsets[2]):
        far2 = far2 + dot(s2[quad_steps.index(dr), 1 + dc], weights[2][i])

    for l in range(3, far_levels):
        pr_count, pc_count = plan.parents[l]
        level_top = tops[l - 3]
        if l == 3:
            for pr in range(pr_count):
                for pc in range(pc_count):
                    for e in range(plan.ne[3]):
                        level_top[1 + pr, 1 + pc, :, 128 * e : 128 * e + 128] = (
                            l3[2 * pr + e, 2 * pc] + l3[2 * pr + e, 2 * pc + 1]
                        )
        else:
            rows_below, cols_below = plan.grid[l]
            for r in range(rows_below):
                below = tops[l - 4][1 + r, 1 : 1 + cols_below].reshape(32 * cols_below, -1)
                lift = dot(below, updup[l - 1, 0 : below.shape[1]])
                for pc in range(pc_count):
                    first, second = lift[64 * pc : 64 * pc + 32], lift[64 * pc + 32 : 64 * pc + 64]
                    e = r % 2
                    level_top[1 + r // 2, 1 + pc, :, 128 * e : 128 * e + 128] = jnp.where(
                        half32 == 0, first, second
                    ).astype(BF16)

    def far_top(l):
        width = 128 * plan.ne[l]
        pr, pc = quad >> (l - 2), y >> (l - 2)
        total = jnp.zeros((32, width), F32)
        for i, (dr, dc) in enumerate(plan.offsets[l]):
            total = total + dot(tops[l - 3][1 + pr + dr, 1 + pc + dc], weights[l][i])
        return total

    local = None
    for l in reversed(range(3, far_levels)):
        total = far_top(l)
        if local is not None:
            total = total + dot(local, downst[l, 0 : local.shape[1], 0 : total.shape[1]])
        child = 2 * ((quad >> (l - 3)) % 2) + (y >> (l - 3)) % 2
        local = jnp.where(halves(total.shape) == child, total, 0.0).astype(BF16)
    total = far2 + dot(local, downst[2, 0 : local.shape[1], 0:256])
    lane = halves(total.shape)
    base = 2 * (g // 2 % 2)
    local = jnp.concatenate([jnp.where(lane == base + f, total, 0.0) for f in (0, 1)], axis=0).astype(BF16)
    total = far1 + dot(local, downst[1])
    base = 2 * (g % 2)
    local = jnp.concatenate(
        [jnp.where(lane == base + f, total[32 * pc : 32 * pc + 32], 0.0) for pc in (0, 1) for f in (0, 1)], axis=0
    ).astype(BF16)
    total = dot(local, downst[0])

    for i, (dr, dc) in enumerate(plan.offsets[0]):
        total = total + dot(s0[1 + dr, 1 + dc : 5 + dc].reshape(128, 256), weights[0][i])
    local = total.astype(BF16)
    local = jnp.concatenate([local[:, 0:128], local[:, 128:256]], axis=0)
    spread = dot(local, basis2[...])

    for e in (0, 1):
        lhs = jnp.concatenate(
            [
                pbuf[1 + e + u, 1 + v : 9 + v].reshape(256, 128)
                for u in (-1, 0, 1)
                for v in (-1, 0, 1)
            ],
            axis=1,
        )
        near = dot(lhs, table[...])
        for b in range(8):
            p, f = b // 2, b % 2
            far = spread[128 * e + 32 * p : 128 * e + 32 * p + 32, 128 * f : 128 * f + 128]
            out[e, b] = (near[32 * b : 32 * b + 32] + far).astype(BF16)

    for copy, valid in sent:
        if valid is None:
            copy.wait_send()
        else:
            pl.when(valid)(copy.wait_send)


def shards(plan, probes, leaf_basis, up_transfer, down_transfer, coupling, far_ids):
    quads, cols_dev, far_levels, top = plan.quads, plan.cols_dev, plan.far_levels, plan.top
    dma = pltpu.SemaphoreType.DMA
    near_count = 4 * (1 if quads == 1 else 3) - 1
    send_count = near_count + 12 + 4 + quads * cols_dev - 1 + 4 + 8
    scratch = [
        pltpu.VMEM((4, 10, 32, 128), BF16),
        pltpu.VMEM((3, 6, 32, 256), BF16),
        pltpu.VMEM((plan.window, 2, 32, 128), BF16),
        pltpu.VMEM((plan.window, 2, 32, 128), BF16),
        pltpu.VMEM((1 if quads == 1 else 3, 3, 32, 256), BF16),
        pltpu.VMEM((quads, cols_dev, 32, 128), BF16),
        pltpu.VMEM((9 * 128, 128), BF16),
        pltpu.VMEM((64, 128), BF16),
        pltpu.SMEM(far_ids.shape, jnp.int32),
        pltpu.VMEM((128, 256), BF16),
        pltpu.VMEM((top, 4, 64, 64), BF16),
        pltpu.VMEM((top, 4, 64, 64), BF16),
        pltpu.VMEM((top, 256, 128), BF16),
        pltpu.VMEM((top, 256, 256), BF16),
    ]
    for l in range(far_levels):
        scratch.append(pltpu.VMEM((len(plan.offsets[l]), 128 * plan.ne[l], 128 * plan.ne[l]), BF16))
    scratch += [pltpu.VMEM(coupling.shape[1:], BF16) for _ in range(far_levels)]
    for l in range(3, far_levels):
        pr, pc = plan.parents[l]
        scratch.append(pltpu.VMEM((pr + 2, pc + 2, 32, 128 * plan.ne[l]), BF16))
    scratch += [
        dma((5 + far_levels,)),
        dma((send_count,)),
        dma((3, 2, 2)),
        dma((2, 2)),
        dma((2, 2, 2)),
        dma((plan.window,)),
        dma((2, 2)),
        dma((quads, cols_dev)),
    ]
    anywhere = pl.BlockSpec(memory_space=pltpu.HBM)
    vmem = pl.BlockSpec(memory_space=pltpu.VMEM)
    return pl.pallas_call(
        functools.partial(kernel, plan),
        out_shape=jax.ShapeDtypeStruct(probes.shape, BF16),
        in_specs=[anywhere] * 6,
        out_specs=vmem,
        scratch_shapes=scratch,
        compiler_params=pltpu.CompilerParams(
            collective_id=0, has_side_effects=True, vmem_limit_bytes=60 * 1024 * 1024
        ),
    )(probes, leaf_basis.T, up_transfer, down_transfer, coupling, far_ids)


def solution(mesh):
    in_specs = (P("gx", "gy", None, None), P(), P(), P(), P(), P())
    out_specs = P("gx", "gy", None, None)

    def run(probes, leaf_basis, up_transfer, down_transfer, coupling, far_ids):
        plan = Plan(mesh.shape["gx"], mesh.shape["gy"], coupling.shape[0])
        return jax.shard_map(
            functools.partial(shards, plan), mesh=mesh, in_specs=in_specs, out_specs=out_specs, check_vma=False
        )(probes, leaf_basis, up_transfer, down_transfer, coupling, far_ids)

    return run
```

```python
import functools

import jax
import jax.numpy as jnp
from jax import lax
from jax.experimental import pallas as pl
from jax.experimental.pallas import tpu as pltpu
from jax.sharding import PartitionSpec as P

LEAF_ROWS = 8
LEAF_COLS = 16
LENGTH_SCALE = 1.5
MESH = pl.DeviceIdType.MESH
BF16 = jnp.bfloat16
F32 = jnp.float32
AROUND = [(du, dv) for du in (-1, 0, 1) for dv in (-1, 0, 1) if (du, dv) != (0, 0)]


def slot_offsets(type_row, type_col):
    offsets = []
    for off_row in range(-2 - type_row, 4 - type_row):
        for off_col in range(-2 - type_col, 4 - type_col):
            if max(abs(off_row), abs(off_col)) > 1:
                offsets.append((off_row, off_col))
    return offsets


SLOT_OF = {
    (e, f): {offset: s for s, offset in enumerate(slot_offsets(e, f))} for e in (0, 1) for f in (0, 1)
}


class Plan:
    def __init__(self, rows_dev, cols_dev, levels):
        self.rows_dev, self.cols_dev, self.levels = rows_dev, cols_dev, levels
        self.quads = rows_dev // 4
        self.pad = 2 if self.quads == 1 else 4
        self.window = 4 + 2 * self.pad
        self.grid = [(max(1, 2 * rows_dev >> l), max(1, 8 * cols_dev >> l)) for l in range(levels)]
        self.parents = [((r + 1) // 2, (c + 1) // 2) for r, c in self.grid]
        self.ne = [2 if r > 1 else 1 for r, _ in self.grid]
        self.offsets = [
            [(dr, dc) for dr, dc in AROUND if (pr > 1 or dr == 0) and (pc > 1 or dc == 0)]
            for pr, pc in self.parents
        ]
        self.top = max(l for l in range(levels) if self.offsets[l])
        self.far_levels = self.top + 1


def dot(a, b):
    return jnp.dot(a, b, preferred_element_type=F32)


def kernel(
    plan, probes, basis, up, down, coupling, ids_hbm, out,
    pbuf, s0, l1, l1side, s2, l3, table, basisv, ids, basis2, upv, downv, updup, downst, *rest,
):
    far_levels, top = plan.far_levels, plan.top
    weights, coup, rest = rest[:far_levels], rest[far_levels : 2 * far_levels], rest[2 * far_levels :]
    tops, rest = rest[: top - 2], rest[top - 2 :]
    local_sem, send_sem, rowrecv, colrecv, cornerrecv, l1recv, siderecv, l3recv = rest
    rows_dev, cols_dev, quads, pad = plan.rows_dev, plan.cols_dev, plan.quads, plan.pad
    g = lax.axis_index("gx")
    y = lax.axis_index("gy")
    quad, member = g // 4, g % 4
    quad_steps = (0,) if quads == 1 else (-1, 0, 1)

    def inside(row, col):
        return (row >= 0) & (row < rows_dev) & (col >= 0) & (col < cols_dev)

    near_partners = [(dq, k) for dq in quad_steps for k in range(4) if (dq, k) != (0, 0)]
    far_partners = [(kq, ky) for kq in range(quads) for ky in range(cols_dev) if (kq, ky) != (0, 0)]

    def near_device(dq, k):
        return (quad + dq) * 4 + (member + k) % 4, y

    def far_device(kq, ky):
        return (quad + kq) % quads * 4 + member, (y + ky) % cols_dev

    def met(row, col):
        return (abs(row // 4 - quad) <= 1) & (col == y)

    barrier = pltpu.get_barrier_semaphore()
    expected = jnp.int32(0)
    for partner in near_partners:
        row, col = near_device(*partner)
        valid = inside(row, col)

        @pl.when(valid)
        def _():
            pl.semaphore_signal(barrier, inc=1, device_id=(row, col), device_id_type=MESH)

        expected = expected + jnp.where(valid, 1, 0)
    for partner in far_partners:
        row, col = far_device(*partner)
        valid = jnp.logical_not(met(row, col))

        @pl.when(valid)
        def _():
            pl.semaphore_signal(barrier, inc=1, device_id=(row, col), device_id_type=MESH)

        expected = expected + jnp.where(valid, 1, 0)

    fetch = [
        pltpu.make_async_copy(probes, pbuf.at[1:3, 1:9], local_sem.at[0]),
        pltpu.make_async_copy(up.at[0:top], upv, local_sem.at[1]),
        pltpu.make_async_copy(down.at[0:top], downv, local_sem.at[2]),
        pltpu.make_async_copy(basis, basisv, local_sem.at[3]),
        pltpu.make_async_copy(ids_hbm, ids, local_sem.at[4]),
    ]
    fetch_coup = [
        pltpu.make_async_copy(coupling.at[l], coup[l], local_sem.at[5 + l]) for l in range(far_levels)
    ]
    for copy in fetch + fetch_coup:
        copy.start()

    def clear(part):
        part[...] = jnp.zeros(part.shape, BF16)

    halo_row = {1: 0, -1: 2}
    probe_row = {1: 0, -1: 3}
    own_adjacent = {1: 2, -1: 1}
    far_half = {1: slice(0, 128), -1: slice(128, 256)}
    near_half = {1: slice(128, 256), -1: slice(0, 128)}
    probe_side = {1: slice(0, 1), -1: slice(9, 10)}
    coef_side = {1: slice(0, 1), -1: slice(5, 6)}
    own_probe_edge = {1: slice(8, 9), -1: slice(1, 2)}
    own_coef_edge = {1: slice(4, 5), -1: slice(1, 2)}
    side_of = {1: 0, -1: 1}
    signs = (1, -1)

    def row_inside(row):
        return (row >= 0) & (row < rows_dev)

    def col_inside(col):
        return (col >= 0) & (col < cols_dev)

    for d in signs:

        @pl.when(jnp.logical_not(row_inside(g - d)))
        def _():
            clear(pbuf.at[probe_row[d]])
            clear(s0.at[halo_row[d]])

        @pl.when(jnp.logical_not(col_inside(y - d)))
        def _():
            clear(pbuf.at[:, probe_side[d]])
            clear(s0.at[:, coef_side[d]])
            clear(l1side.at[:, side_of[d]])
            clear(s2.at[:, 1 - d])

    if quads == 1:
        for part in (l1, l1side):
            clear(part.at[0:pad])
            clear(part.at[pad + 4 : 2 * pad + 4])
    else:

        @pl.when(quad == 0)
        def _():
            clear(l1.at[0:4])

        @pl.when(quad == quads - 1)
        def _():
            clear(l1.at[8:12])

    for level_top in tops:
        clear(level_top)

    basis2[...] = jnp.zeros((128, 256), BF16)
    fetch[3].wait()
    basis2[0:64, 0:128] = basisv[...]
    basis2[64:128, 128:256] = basisv[...]

    fetch[1].wait()

    def make_updup(l):
        width = plan.ne[l] * 128
        wide = upv[l, 0 : 2 * plan.ne[l]].reshape(width, 64)
        updup[l, 0:width] = jnp.concatenate([wide, wide], axis=1)

    make_updup(0)
    fetch[0].wait()
    left_rows = jnp.concatenate(
        [
            jnp.concatenate([pbuf[1 + e, 1 + 2 * p], pbuf[1 + e, 2 + 2 * p]], axis=1)
            for e in (0, 1)
            for p in range(4)
        ],
        axis=0,
    )
    leaf = lax.dot_general(
        left_rows, basis2[...], (((1,), (1,)), ((), ())), preferred_element_type=F32
    ).astype(BF16)
    own = jnp.concatenate([leaf[0:128], leaf[128:256]], axis=1)
    s0[1, 1:5] = own.reshape(4, 32, 256)

    def halves(shape):
        return lax.broadcasted_iota(jnp.int32, shape, len(shape) - 1) // 64

    half32 = halves((32, 128))
    lifted = dot(own, updup[0, 0:256])
    own_row = pad + member
    for pc in (0, 1):
        first = lifted[64 * pc : 64 * pc + 32]
        second = lifted[64 * pc + 32 : 64 * pc + 64]
        l1[own_row, pc] = jnp.where(half32 == 0, first, second).astype(BF16)

    pl.semaphore_wait(barrier, expected)

    sent = []

    def send(src, dst, recv, device, valid):
        copy = pltpu.make_async_remote_copy(
            src_ref=src, dst_ref=dst, send_sem=send_sem.at[len(sent)], recv_sem=recv,
            device_id=device, device_id_type=MESH,
        )
        sent.append((copy, valid))
        if valid is None:
            copy.start()
        else:
            pl.when(valid)(copy.start)

    def receive(dst, recv, valid):
        copy = pltpu.make_async_remote_copy(
            src_ref=dst, dst_ref=dst, send_sem=send_sem.at[0], recv_sem=recv,
            device_id=(g, y), device_id_type=MESH,
        )
        if valid is None:
            copy.wait_recv()
        else:
            pl.when(valid)(copy.wait_recv)

    ordered = sorted(near_partners, key=lambda t: abs(t[0]))
    for dq, k in ordered:
        device = near_device(dq, k)
        row = pad - 4 * dq + member
        valid = None if dq == 0 else inside(*device)
        send(l1.at[own_row], l1.at[row], l1recv.at[row], device, valid)

    pieces = [(slice(1, 3), slice(1, 2)), (slice(7, 9), slice(4, 5)), (slice(3, 7), slice(2, 4))]

    def send_rows(piece):
        probe_cols, coef_cols = pieces[piece]
        for d in signs:
            device, valid = (g + d, y), row_inside(g + d)
            send(
                s0.at[1, coef_cols, :, far_half[d]], s0.at[halo_row[d], coef_cols, :, far_half[d]],
                rowrecv.at[piece, side_of[d], 0], device, valid,
            )
            send(
                pbuf.at[own_adjacent[d], probe_cols], pbuf.at[probe_row[d], probe_cols],
                rowrecv.at[piece, side_of[d], 1], device, valid,
            )

    def receive_rows(piece):
        probe_cols, coef_cols = pieces[piece]
        for d in signs:
            valid = row_inside(g - d)
            receive(s0.at[halo_row[d], coef_cols, :, far_half[d]], rowrecv.at[piece, side_of[d], 0], valid)
            receive(pbuf.at[probe_row[d], probe_cols], rowrecv.at[piece, side_of[d], 1], valid)

    send_rows(0)
    send_rows(1)
    for d in signs:
        device, valid = (g, y + d), col_inside(y + d)
        send(s0.at[1, own_coef_edge[d]], s0.at[1, coef_side[d]], colrecv.at[side_of[d], 0], device, valid)
        send(
            pbuf.at[1:3, own_probe_edge[d]], pbuf.at[1:3, probe_side[d]], colrecv.at[side_of[d], 1], device, valid
        )
    send_rows(2)

    for l in range(1, top):
        make_updup(l)

    point_q = lax.broadcasted_iota(jnp.int32, (128, 128), 0)
    point_p = lax.broadcasted_iota(jnp.int32, (128, 128), 1)
    row_apart = (point_q // LEAF_COLS - point_p // LEAF_COLS).astype(F32)
    col_apart = (point_q % LEAF_COLS - point_p % LEAF_COLS).astype(F32)
    for i, (u, v) in enumerate([(u, v) for u in (-1, 0, 1) for v in (-1, 0, 1)]):
        dr = row_apart + float(u * LEAF_ROWS)
        dc = col_apart + float(v * LEAF_COLS)
        t = jnp.sqrt(3.0 * (dr * dr + dc * dc)) / LENGTH_SCALE
        table[128 * i : 128 * i + 128] = ((1.0 + t) * jnp.exp(-t)).astype(BF16)

    for dq, k in ordered:
        row = pad + 4 * dq + (member + k) % 4
        receive(l1.at[row], l1recv.at[row], None if dq == 0 else inside(*near_device(dq, k)))
    parts = []
    for dq in quad_steps:
        for e in (0, 1):
            for pc in (0, 1):
                row = pad + 4 * dq + 2 * e
                parts.append(jnp.concatenate([l1[row, pc], l1[row + 1, pc]], axis=1))
    lift = dot(jnp.concatenate(parts, axis=0), updup[1, 0:256])
    for i, dq in enumerate(quad_steps):
        both = []
        for e in (0, 1):
            at = 128 * i + 64 * e
            both.append(jnp.where(half32 == 0, lift[at : at + 32], lift[at + 32 : at + 64]))
        s2[i, 1] = jnp.concatenate(both, axis=1).astype(BF16)
    lift = dot(s2[quad_steps.index(0), 1], updup[2, 0:256])
    l3[quad, y] = jnp.where(half32 == y % 2, lift, 0.0).astype(BF16)
    for kq, ky in far_partners:
        device = far_device(kq, ky)
        send(l3.at[quad, y], l3.at[quad, y], l3recv.at[quad, y], device, None)
    rows_sent = slice(pad, pad + 4) if quads == 1 else slice(0, plan.window)
    for d in signs:
        device, valid = (g, y + d), col_inside(y + d)
        send(l1.at[rows_sent, (1 + d) // 2], l1side.at[rows_sent, side_of[d]], siderecv.at[side_of[d], 0], device, valid)
        send(s2.at[:, 1], s2.at[:, 1 - d], siderecv.at[side_of[d], 1], device, valid)

    def adjacent(parents):
        rows = [
            jnp.concatenate([pbuf[probe_row[d], 2 * p - 1], pbuf[probe_row[d], 2 * p]], axis=1)
            for d in signs
            for p in parents
        ]
        coefs = lax.dot_general(
            jnp.concatenate(rows, axis=0), basis2[...], (((1,), (1,)), ((), ())), preferred_element_type=F32
        ).astype(BF16)
        at = 0
        for d in signs:
            for p in parents:
                s0[halo_row[d], p, :, near_half[d]] = coefs[at : at + 32]
                at += 32

    receive_rows(0)
    receive_rows(1)
    adjacent((1, 4))
    for d in signs:
        for v in signs:
            device, valid = (g, y + v), row_inside(g - d) & col_inside(y + v)
            send(
                s0.at[halo_row[d], own_coef_edge[v]], s0.at[halo_row[d], coef_side[v]],
                cornerrecv.at[side_of[d], side_of[v], 0], device, valid,
            )
            send(
                pbuf.at[probe_row[d], own_probe_edge[v]], pbuf.at[probe_row[d], probe_side[v]],
                cornerrecv.at[side_of[d], side_of[v], 1], device, valid,
            )

    fetch[2].wait()
    for l in range(top):
        for e in range(plan.ne[l]):
            wide = jnp.concatenate([downv[l, 2 * e], downv[l, 2 * e + 1]], axis=1)
            for c in range(2 * plan.ne[l + 1]):
                downst[l, 64 * c : 64 * c + 64, 128 * e : 128 * e + 128] = wide

    empty = jnp.zeros((64, 64), BF16)
    fetch[4].wait()
    for l in reversed(range(far_levels)):
        fetch_coup[l].wait()
        for i, (dr, dc) in enumerate(plan.offsets[l]):
            for se in range(plan.ne[l]):
                for sf in (0, 1):
                    for e in range(plan.ne[l]):
                        pair = []
                        for f in (0, 1):
                            slot = SLOT_OF[e, f].get((2 * dr + se - e, 2 * dc + sf - f))
                            pair.append(empty if slot is None else coup[l][ids[l, 2 * e + f, slot]])
                        c = 2 * se + sf
                        weights[l][i, 64 * c : 64 * c + 64, 128 * e : 128 * e + 128] = jnp.concatenate(pair, axis=1)

    for d in signs:
        valid = col_inside(y - d)
        receive(l1side.at[rows_sent, side_of[d]], siderecv.at[side_of[d], 0], valid)
        receive(s2.at[:, 1 - d], siderecv.at[side_of[d], 1], valid)
        receive(s0.at[1, coef_side[d]], colrecv.at[side_of[d], 0], valid)
        receive(pbuf.at[1:3, probe_side[d]], colrecv.at[side_of[d], 1], valid)
    for kq, ky in far_partners:
        row, col = (quad + kq) % quads, (y + ky) % cols_dev
        receive(l3.at[row, col], l3recv.at[row, col], None)
    receive_rows(2)
    for d in signs:
        for v in signs:
            valid = row_inside(g - d) & col_inside(y - v)
            receive(s0.at[halo_row[d], coef_side[v]], cornerrecv.at[side_of[d], side_of[v], 0], valid)
            receive(pbuf.at[probe_row[d], probe_side[v]], cornerrecv.at[side_of[d], side_of[v], 1], valid)
    adjacent((2, 3))

    pair_row = pad + 2 * (member // 2)
    far1 = jnp.zeros((64, 256), F32)
    for dr in (-1, 0, 1):
        row = pair_row + 2 * dr
        tiles = [
            jnp.concatenate([ref[row, at], ref[row + 1, at]], axis=1)
            for ref, at in ((l1side, 0), (l1, 0), (l1, 1), (l1side, 1))
        ]
        for dc in (-1, 0, 1):
            if (dr, dc) in plan.offsets[1]:
                lhs = jnp.concatenate([tiles[1 + dc], tiles[2 + dc]], axis=0)
                far1 = far1 + dot(lhs, weights[1][plan.offsets[1].index((dr, dc))])
    far2 = jnp.zeros((32, 256), F32)
    for i, (dr, dc) in enumerate(plan.offsets[2]):
        far2 = far2 + dot(s2[quad_steps.index(dr), 1 + dc], weights[2][i])

    for l in range(3, far_levels):
        pr_count, pc_count = plan.parents[l]
        level_top = tops[l - 3]
        if l == 3:
            for pr in range(pr_count):
                for pc in range(pc_count):
                    for e in range(plan.ne[3]):
                        level_top[1 + pr, 1 + pc, :, 128 * e : 128 * e + 128] = (
                            l3[2 * pr + e, 2 * pc] + l3[2 * pr + e, 2 * pc + 1]
                        )
        else:
            rows_below, cols_below = plan.grid[l]
            for r in range(rows_below):
                below = tops[l - 4][1 + r, 1 : 1 + cols_below].reshape(32 * cols_below, -1)
                lift = dot(below, updup[l - 1, 0 : below.shape[1]])
                for pc in range(pc_count):
                    first, second = lift[64 * pc : 64 * pc + 32], lift[64 * pc + 32 : 64 * pc + 64]
                    e = r % 2
                    level_top[1 + r // 2, 1 + pc, :, 128 * e : 128 * e + 128] = jnp.where(
                        half32 == 0, first, second
                    ).astype(BF16)

    def far_top(l):
        width = 128 * plan.ne[l]
        pr, pc = quad >> (l - 2), y >> (l - 2)
        total = jnp.zeros((32, width), F32)
        for i, (dr, dc) in enumerate(plan.offsets[l]):
            total = total + dot(tops[l - 3][1 + pr + dr, 1 + pc + dc], weights[l][i])
        return total

    local = None
    for l in reversed(range(3, far_levels)):
        total = far_top(l)
        if local is not None:
            total = total + dot(local, downst[l, 0 : local.shape[1], 0 : total.shape[1]])
        child = 2 * ((quad >> (l - 3)) % 2) + (y >> (l - 3)) % 2
        local = jnp.where(halves(total.shape) == child, total, 0.0).astype(BF16)
    total = far2 + dot(local, downst[2, 0 : local.shape[1], 0:256])
    lane = halves(total.shape)
    base = 2 * (g // 2 % 2)
    local = jnp.concatenate([jnp.where(lane == base + f, total, 0.0) for f in (0, 1)], axis=0).astype(BF16)
    total = far1 + dot(local, downst[1])
    base = 2 * (g % 2)
    local = jnp.concatenate(
        [jnp.where(lane == base + f, total[32 * pc : 32 * pc + 32], 0.0) for pc in (0, 1) for f in (0, 1)], axis=0
    ).astype(BF16)
    total = dot(local, downst[0])

    for i, (dr, dc) in enumerate(plan.offsets[0]):
        total = total + dot(s0[1 + dr, 1 + dc : 5 + dc].reshape(128, 256), weights[0][i])
    local = total.astype(BF16)
    local = jnp.concatenate([local[:, 0:128], local[:, 128:256]], axis=0)
    spread = dot(local, basis2[...])

    for e in (0, 1):
        lhs = jnp.concatenate(
            [
                pbuf[1 + e + u, 1 + v : 9 + v].reshape(256, 128)
                for u in (-1, 0, 1)
                for v in (-1, 0, 1)
            ],
            axis=1,
        )
        near = dot(lhs, table[...])
        for b in range(8):
            p, f = b // 2, b % 2
            far = spread[128 * e + 32 * p : 128 * e + 32 * p + 32, 128 * f : 128 * f + 128]
            out[e, b] = (near[32 * b : 32 * b + 32] + far).astype(BF16)

    for copy, valid in sent:
        if valid is None:
            copy.wait_send()
        else:
            pl.when(valid)(copy.wait_send)


def shards(plan, probes, leaf_basis, up_transfer, down_transfer, coupling, far_ids):
    quads, cols_dev, far_levels, top = plan.quads, plan.cols_dev, plan.far_levels, plan.top
    dma = pltpu.SemaphoreType.DMA
    near_count = 4 * (1 if quads == 1 else 3) - 1
    send_count = near_count + 12 + 4 + quads * cols_dev - 1 + 4 + 8
    scratch = [
        pltpu.VMEM((4, 10, 32, 128), BF16),
        pltpu.VMEM((3, 6, 32, 256), BF16),
        pltpu.VMEM((plan.window, 2, 32, 128), BF16),
        pltpu.VMEM((plan.window, 2, 32, 128), BF16),
        pltpu.VMEM((1 if quads == 1 else 3, 3, 32, 256), BF16),
        pltpu.VMEM((quads, cols_dev, 32, 128), BF16),
        pltpu.VMEM((9 * 128, 128), BF16),
        pltpu.VMEM((64, 128), BF16),
        pltpu.SMEM(far_ids.shape, jnp.int32),
        pltpu.VMEM((128, 256), BF16),
        pltpu.VMEM((top, 4, 64, 64), BF16),
        pltpu.VMEM((top, 4, 64, 64), BF16),
        pltpu.VMEM((top, 256, 128), BF16),
        pltpu.VMEM((top, 256, 256), BF16),
    ]
    for l in range(far_levels):
        scratch.append(pltpu.VMEM((len(plan.offsets[l]), 128 * plan.ne[l], 128 * plan.ne[l]), BF16))
    scratch += [pltpu.VMEM(coupling.shape[1:], BF16) for _ in range(far_levels)]
    for l in range(3, far_levels):
        pr, pc = plan.parents[l]
        scratch.append(pltpu.VMEM((pr + 2, pc + 2, 32, 128 * plan.ne[l]), BF16))
    scratch += [
        dma((5 + far_levels,)),
        dma((send_count,)),
        dma((3, 2, 2)),
        dma((2, 2)),
        dma((2, 2, 2)),
        dma((plan.window,)),
        dma((2, 2)),
        dma((quads, cols_dev)),
    ]
    anywhere = pl.BlockSpec(memory_space=pltpu.HBM)
    vmem = pl.BlockSpec(memory_space=pltpu.VMEM)
    operands = [
        pltpu.with_memory_space_constraint(x, pltpu.HBM)
        for x in (probes, leaf_basis.T, up_transfer, down_transfer, coupling, far_ids)
    ]
    return pl.pallas_call(
        functools.partial(kernel, plan),
        out_shape=jax.ShapeDtypeStruct(probes.shape, BF16),
        in_specs=[anywhere] * 6,
        out_specs=vmem,
        scratch_shapes=scratch,
        compiler_params=pltpu.CompilerParams(
            collective_id=0, has_side_effects=True, vmem_limit_bytes=40 * 1024 * 1024
        ),
    )(*operands)


def solution(mesh):
    in_specs = (P("gx", "gy", None, None), P(), P(), P(), P(), P())
    out_specs = P("gx", "gy", None, None)

    def run(probes, leaf_basis, up_transfer, down_transfer, coupling, far_ids):
        plan = Plan(mesh.shape["gx"], mesh.shape["gy"], coupling.shape[0])
        return jax.shard_map(
            functools.partial(shards, plan), mesh=mesh, in_specs=in_specs, out_specs=out_specs, check_vma=False
        )(probes, leaf_basis, up_transfer, down_transfer, coupling, far_ids)

    return run
```

```python
import functools

import jax
import jax.numpy as jnp
from jax import lax
from jax.experimental import pallas as pl
from jax.experimental.pallas import tpu as pltpu
from jax.sharding import PartitionSpec as P

LEAF_ROWS = 8
LEAF_COLS = 16
LENGTH_SCALE = 1.5
MESH = pl.DeviceIdType.MESH
BF16 = jnp.bfloat16
F32 = jnp.float32
AROUND = [(du, dv) for du in (-1, 0, 1) for dv in (-1, 0, 1) if (du, dv) != (0, 0)]


def slot_offsets(type_row, type_col):
    offsets = []
    for off_row in range(-2 - type_row, 4 - type_row):
        for off_col in range(-2 - type_col, 4 - type_col):
            if max(abs(off_row), abs(off_col)) > 1:
                offsets.append((off_row, off_col))
    return offsets


SLOT_OF = {
    (e, f): {offset: s for s, offset in enumerate(slot_offsets(e, f))} for e in (0, 1) for f in (0, 1)
}


class Plan:
    def __init__(self, rows_dev, cols_dev, levels):
        self.rows_dev, self.cols_dev, self.levels = rows_dev, cols_dev, levels
        self.quads = rows_dev // 4
        self.pad = 2 if self.quads == 1 else 4
        self.window = 4 + 2 * self.pad
        self.grid = [(max(1, 2 * rows_dev >> l), max(1, 8 * cols_dev >> l)) for l in range(levels)]
        self.parents = [((r + 1) // 2, (c + 1) // 2) for r, c in self.grid]
        self.ne = [2 if r > 1 else 1 for r, _ in self.grid]
        self.offsets = [
            [(dr, dc) for dr, dc in AROUND if (pr > 1 or dr == 0) and (pc > 1 or dc == 0)]
            for pr, pc in self.parents
        ]
        self.top = max(l for l in range(levels) if self.offsets[l])
        self.far_levels = self.top + 1


def dot(a, b):
    return jnp.dot(a, b, preferred_element_type=F32)


def kernel(
    plan, probes, basis, up, down, coupling, ids_hbm, out,
    pbuf, s0, l1, l1side, s2, l3, table, basisv, ids, basis2, upv, downv, updup, downst, *rest,
):
    far_levels, top = plan.far_levels, plan.top
    weights, coup, rest = rest[:far_levels], rest[far_levels : 2 * far_levels], rest[2 * far_levels :]
    tops, rest = rest[: top - 2], rest[top - 2 :]
    local_sem, send_sem, rowrecv, colrecv, cornerrecv, l1recv, siderecv, l3recv = rest
    rows_dev, cols_dev, quads, pad = plan.rows_dev, plan.cols_dev, plan.quads, plan.pad
    g = lax.axis_index("gx")
    y = lax.axis_index("gy")
    quad, member = g // 4, g % 4
    quad_steps = (0,) if quads == 1 else (-1, 0, 1)

    def inside(row, col):
        return (row >= 0) & (row < rows_dev) & (col >= 0) & (col < cols_dev)

    near_partners = [(dq, k) for dq in quad_steps for k in range(4) if (dq, k) != (0, 0)]
    far_partners = [(kq, ky) for kq in range(quads) for ky in range(cols_dev) if (kq, ky) != (0, 0)]

    def near_device(dq, k):
        return (quad + dq) * 4 + (member + k) % 4, y

    def far_device(kq, ky):
        return (quad + kq) % quads * 4 + member, (y + ky) % cols_dev

    def met(row, col):
        return (abs(row // 4 - quad) <= 1) & (col == y)

    barrier = pltpu.get_barrier_semaphore()
    expected = jnp.int32(0)
    for partner in near_partners:
        row, col = near_device(*partner)
        valid = inside(row, col)

        @pl.when(valid)
        def _():
            pl.semaphore_signal(barrier, inc=1, device_id=(row, col), device_id_type=MESH)

        expected = expected + jnp.where(valid, 1, 0)
    for partner in far_partners:
        row, col = far_device(*partner)
        valid = jnp.logical_not(met(row, col))

        @pl.when(valid)
        def _():
            pl.semaphore_signal(barrier, inc=1, device_id=(row, col), device_id_type=MESH)

        expected = expected + jnp.where(valid, 1, 0)

    fetch = [
        pltpu.make_async_copy(probes, pbuf.at[1:3, 1:9], local_sem.at[0]),
        pltpu.make_async_copy(up.at[0:top], upv, local_sem.at[1]),
        pltpu.make_async_copy(down.at[0:top], downv, local_sem.at[2]),
        pltpu.make_async_copy(basis, basisv, local_sem.at[3]),
        pltpu.make_async_copy(ids_hbm, ids, local_sem.at[4]),
    ]
    fetch_coup = [
        pltpu.make_async_copy(coupling.at[l], coup[l], local_sem.at[5 + l]) for l in range(far_levels)
    ]
    for at in (3, 0, 1, 4, 2):
        fetch[at].start()
    for copy in reversed(fetch_coup):
        copy.start()

    def clear(part):
        part[...] = jnp.zeros(part.shape, BF16)

    halo_row = {1: 0, -1: 2}
    probe_row = {1: 0, -1: 3}
    own_adjacent = {1: 2, -1: 1}
    far_half = {1: slice(0, 128), -1: slice(128, 256)}
    near_half = {1: slice(128, 256), -1: slice(0, 128)}
    probe_side = {1: slice(0, 1), -1: slice(9, 10)}
    coef_side = {1: slice(0, 1), -1: slice(5, 6)}
    own_probe_edge = {1: slice(8, 9), -1: slice(1, 2)}
    own_coef_edge = {1: slice(4, 5), -1: slice(1, 2)}
    side_of = {1: 0, -1: 1}
    signs = (1, -1)

    def row_inside(row):
        return (row >= 0) & (row < rows_dev)

    def col_inside(col):
        return (col >= 0) & (col < cols_dev)

    for d in signs:

        @pl.when(jnp.logical_not(row_inside(g - d)))
        def _():
            clear(pbuf.at[probe_row[d]])
            clear(s0.at[halo_row[d]])

        @pl.when(jnp.logical_not(col_inside(y - d)))
        def _():
            clear(pbuf.at[:, probe_side[d]])
            clear(s0.at[:, coef_side[d]])
            clear(l1side.at[:, side_of[d]])
            clear(s2.at[:, 1 - d])

    if quads == 1:
        for part in (l1, l1side):
            clear(part.at[0:pad])
            clear(part.at[pad + 4 : 2 * pad + 4])
    else:

        @pl.when(quad == 0)
        def _():
            clear(l1.at[0:4])

        @pl.when(quad == quads - 1)
        def _():
            clear(l1.at[8:12])

    for level_top in tops:
        clear(level_top)

    point_q = lax.broadcasted_iota(jnp.int32, (128, 128), 0)
    point_p = lax.broadcasted_iota(jnp.int32, (128, 128), 1)
    row_apart = (point_q // LEAF_COLS - point_p // LEAF_COLS).astype(F32)
    col_apart = (point_q % LEAF_COLS - point_p % LEAF_COLS).astype(F32)
    for i, (u, v) in enumerate([(u, v) for u in (-1, 0, 1) for v in (-1, 0, 1)]):
        dr = row_apart + float(u * LEAF_ROWS)
        dc = col_apart + float(v * LEAF_COLS)
        t = jnp.sqrt(3.0 * (dr * dr + dc * dc)) / LENGTH_SCALE
        table[128 * i : 128 * i + 128] = ((1.0 + t) * jnp.exp(-t)).astype(BF16)

    basis2[...] = jnp.zeros((128, 256), BF16)
    fetch[3].wait()
    basis2[0:64, 0:128] = basisv[...]
    basis2[64:128, 128:256] = basisv[...]

    fetch[1].wait()

    def make_updup(l):
        width = plan.ne[l] * 128
        wide = upv[l, 0 : 2 * plan.ne[l]].reshape(width, 64)
        updup[l, 0:width] = jnp.concatenate([wide, wide], axis=1)

    make_updup(0)
    fetch[0].wait()
    left_rows = jnp.concatenate(
        [
            jnp.concatenate([pbuf[1 + e, 1 + 2 * p], pbuf[1 + e, 2 + 2 * p]], axis=1)
            for e in (0, 1)
            for p in range(4)
        ],
        axis=0,
    )
    leaf = lax.dot_general(
        left_rows, basis2[...], (((1,), (1,)), ((), ())), preferred_element_type=F32
    ).astype(BF16)
    own = jnp.concatenate([leaf[0:128], leaf[128:256]], axis=1)
    s0[1, 1:5] = own.reshape(4, 32, 256)

    def halves(shape):
        return lax.broadcasted_iota(jnp.int32, shape, len(shape) - 1) // 64

    half32 = halves((32, 128))
    lifted = dot(own, updup[0, 0:256])
    own_row = pad + member
    for pc in (0, 1):
        first = lifted[64 * pc : 64 * pc + 32]
        second = lifted[64 * pc + 32 : 64 * pc + 64]
        l1[own_row, pc] = jnp.where(half32 == 0, first, second).astype(BF16)

    pl.semaphore_wait(barrier, expected)

    sent = []
    count = [0]

    def send(valid, parts):
        copies = []
        for src, dst, recv, device in parts:
            copies.append(
                pltpu.make_async_remote_copy(
                    src_ref=src, dst_ref=dst, send_sem=send_sem.at[count[0]], recv_sem=recv,
                    device_id=device, device_id_type=MESH,
                )
            )
            count[0] += 1
        sent.append((valid, copies))

        def start():
            for copy in copies:
                copy.start()

        start() if valid is None else pl.when(valid)(start)

    def receive(valid, parts):
        def wait():
            for dst, recv in parts:
                pltpu.make_async_remote_copy(
                    src_ref=dst, dst_ref=dst, send_sem=send_sem.at[0], recv_sem=recv,
                    device_id=(g, y), device_id_type=MESH,
                ).wait_recv()

        wait() if valid is None else pl.when(valid)(wait)

    def row_parts(d, piece):
        probe_cols, coef_cols = pieces[piece]
        return [
            (
                s0.at[1, coef_cols, :, far_half[d]], s0.at[halo_row[d], coef_cols, :, far_half[d]],
                rowrecv.at[piece, side_of[d], 0], (g + d, y),
            ),
            (
                pbuf.at[own_adjacent[d], probe_cols], pbuf.at[probe_row[d], probe_cols],
                rowrecv.at[piece, side_of[d], 1], (g + d, y),
            ),
        ]

    def arrivals(parts):
        return [(dst, recv) for _, dst, recv, _ in parts]

    for dq in sorted(quad_steps, key=abs):
        valid = None if dq == 0 else (quad + dq >= 0) & (quad + dq < quads)
        row = pad - 4 * dq + member
        send(valid, [
            (l1.at[own_row], l1.at[row], l1recv.at[row], near_device(q, k)) for q, k in near_partners if q == dq
        ])

    pieces = [(slice(1, 3), slice(1, 2)), (slice(7, 9), slice(4, 5)), (slice(3, 7), slice(2, 4))]
    for d in signs:
        send(row_inside(g + d), row_parts(d, 0) + row_parts(d, 1))

    def col_parts(d):
        return [
            (s0.at[1, own_coef_edge[d]], s0.at[1, coef_side[d]], colrecv.at[side_of[d], 0], (g, y + d)),
            (pbuf.at[1:3, own_probe_edge[d]], pbuf.at[1:3, probe_side[d]], colrecv.at[side_of[d], 1], (g, y + d)),
        ]

    for d in signs:
        send(col_inside(y + d), col_parts(d))
    for d in signs:
        send(row_inside(g + d), row_parts(d, 2))

    for l in range(1, top):
        make_updup(l)

    fetch[2].wait()
    for l in range(top):
        for e in range(plan.ne[l]):
            wide = jnp.concatenate([downv[l, 2 * e], downv[l, 2 * e + 1]], axis=1)
            for c in range(2 * plan.ne[l + 1]):
                downst[l, 64 * c : 64 * c + 64, 128 * e : 128 * e + 128] = wide

    empty = jnp.zeros((64, 64), BF16)

    def assemble(l):
        fetch_coup[l].wait()
        for i, (dr, dc) in enumerate(plan.offsets[l]):
            for se in range(plan.ne[l]):
                for sf in (0, 1):
                    for e in range(plan.ne[l]):
                        pair = []
                        for f in (0, 1):
                            slot = SLOT_OF[e, f].get((2 * dr + se - e, 2 * dc + sf - f))
                            pair.append(empty if slot is None else coup[l][ids[l, 2 * e + f, slot]])
                        c = 2 * se + sf
                        weights[l][i, 64 * c : 64 * c + 64, 128 * e : 128 * e + 128] = jnp.concatenate(pair, axis=1)

    fetch[4].wait()
    for l in reversed(range(2, far_levels)):
        assemble(l)

    for dq in sorted(quad_steps, key=abs):
        valid = None if dq == 0 else (quad + dq >= 0) & (quad + dq < quads)
        rows = [pad + 4 * dq + (member + k) % 4 for q, k in near_partners if q == dq]
        receive(valid, [(l1.at[row], l1recv.at[row]) for row in rows])
    parts = []
    for dq in quad_steps:
        for e in (0, 1):
            for pc in (0, 1):
                row = pad + 4 * dq + 2 * e
                parts.append(jnp.concatenate([l1[row, pc], l1[row + 1, pc]], axis=1))
    lift = dot(jnp.concatenate(parts, axis=0), updup[1, 0:256])
    for i, dq in enumerate(quad_steps):
        both = []
        for e in (0, 1):
            at = 128 * i + 64 * e
            both.append(jnp.where(half32 == 0, lift[at : at + 32], lift[at + 32 : at + 64]))
        s2[i, 1] = jnp.concatenate(both, axis=1).astype(BF16)
    lift = dot(s2[quad_steps.index(0), 1], updup[2, 0:256])
    l3[quad, y] = jnp.where(half32 == y % 2, lift, 0.0).astype(BF16)
    send(None, [
        (l3.at[quad, y], l3.at[quad, y], l3recv.at[quad, y], far_device(kq, ky)) for kq, ky in far_partners
    ])
    rows_sent = slice(pad, pad + 4) if quads == 1 else slice(0, plan.window)

    def side_parts(d):
        return [
            (l1.at[rows_sent, (1 + d) // 2], l1side.at[rows_sent, side_of[d]], siderecv.at[side_of[d], 0], (g, y + d)),
            (s2.at[:, 1], s2.at[:, 1 - d], siderecv.at[side_of[d], 1], (g, y + d)),
        ]

    for d in signs:
        send(col_inside(y + d), side_parts(d))

    def adjacent(parents):
        rows = [
            jnp.concatenate([pbuf[probe_row[d], 2 * p - 1], pbuf[probe_row[d], 2 * p]], axis=1)
            for d in signs
            for p in parents
        ]
        coefs = lax.dot_general(
            jnp.concatenate(rows, axis=0), basis2[...], (((1,), (1,)), ((), ())), preferred_element_type=F32
        ).astype(BF16)
        at = 0
        for d in signs:
            for p in parents:
                s0[halo_row[d], p, :, near_half[d]] = coefs[at : at + 32]
                at += 32

    def corner_parts(d, v):
        return [
            (
                s0.at[halo_row[d], own_coef_edge[v]], s0.at[halo_row[d], coef_side[v]],
                cornerrecv.at[side_of[d], side_of[v], 0], (g, y + v),
            ),
            (
                pbuf.at[probe_row[d], own_probe_edge[v]], pbuf.at[probe_row[d], probe_side[v]],
                cornerrecv.at[side_of[d], side_of[v], 1], (g, y + v),
            ),
        ]

    for d in signs:
        receive(row_inside(g - d), arrivals(row_parts(d, 0) + row_parts(d, 1)))
    adjacent((1, 4))
    for d in signs:
        for v in signs:
            send(row_inside(g - d) & col_inside(y + v), corner_parts(d, v))

    assemble(1)
    assemble(0)

    receive(None, [
        (l3.at[row, col], l3recv.at[row, col])
        for row, col in [((quad + kq) % quads, (y + ky) % cols_dev) for kq, ky in far_partners]
    ])
    for d in signs:
        receive(col_inside(y - d), arrivals(side_parts(d) + col_parts(d)))
    for d in signs:
        receive(row_inside(g - d), arrivals(row_parts(d, 2)))
    for d in signs:
        for v in signs:
            receive(row_inside(g - d) & col_inside(y - v), arrivals(corner_parts(d, v)))
    adjacent((2, 3))

    pair_row = pad + 2 * (member // 2)
    far1 = jnp.zeros((64, 256), F32)
    for dr in (-1, 0, 1):
        row = pair_row + 2 * dr
        tiles = [
            jnp.concatenate([ref[row, at], ref[row + 1, at]], axis=1)
            for ref, at in ((l1side, 0), (l1, 0), (l1, 1), (l1side, 1))
        ]
        for dc in (-1, 0, 1):
            if (dr, dc) in plan.offsets[1]:
                lhs = jnp.concatenate([tiles[1 + dc], tiles[2 + dc]], axis=0)
                far1 = far1 + dot(lhs, weights[1][plan.offsets[1].index((dr, dc))])
    far2 = jnp.zeros((32, 256), F32)
    for i, (dr, dc) in enumerate(plan.offsets[2]):
        far2 = far2 + dot(s2[quad_steps.index(dr), 1 + dc], weights[2][i])

    for l in range(3, far_levels):
        pr_count, pc_count = plan.parents[l]
        level_top = tops[l - 3]
        if l == 3:
            for pr in range(pr_count):
                for pc in range(pc_count):
                    for e in range(plan.ne[3]):
                        level_top[1 + pr, 1 + pc, :, 128 * e : 128 * e + 128] = (
                            l3[2 * pr + e, 2 * pc] + l3[2 * pr + e, 2 * pc + 1]
                        )
        else:
            rows_below, cols_below = plan.grid[l]
            for r in range(rows_below):
                below = tops[l - 4][1 + r, 1 : 1 + cols_below].reshape(32 * cols_below, -1)
                lift = dot(below, updup[l - 1, 0 : below.shape[1]])
                for pc in range(pc_count):
                    first, second = lift[64 * pc : 64 * pc + 32], lift[64 * pc + 32 : 64 * pc + 64]
                    e = r % 2
                    level_top[1 + r // 2, 1 + pc, :, 128 * e : 128 * e + 128] = jnp.where(
                        half32 == 0, first, second
                    ).astype(BF16)

    def far_top(l):
        width = 128 * plan.ne[l]
        pr, pc = quad >> (l - 2), y >> (l - 2)
        total = jnp.zeros((32, width), F32)
        for i, (dr, dc) in enumerate(plan.offsets[l]):
            total = total + dot(tops[l - 3][1 + pr + dr, 1 + pc + dc], weights[l][i])
        return total

    local = None
    for l in reversed(range(3, far_levels)):
        total = far_top(l)
        if local is not None:
            total = total + dot(local, downst[l, 0 : local.shape[1], 0 : total.shape[1]])
        child = 2 * ((quad >> (l - 3)) % 2) + (y >> (l - 3)) % 2
        local = jnp.where(halves(total.shape) == child, total, 0.0).astype(BF16)
    total = far2 + dot(local, downst[2, 0 : local.shape[1], 0:256])
    lane = halves(total.shape)
    base = 2 * (g // 2 % 2)
    local = jnp.concatenate([jnp.where(lane == base + f, total, 0.0) for f in (0, 1)], axis=0).astype(BF16)
    total = far1 + dot(local, downst[1])
    base = 2 * (g % 2)
    local = jnp.concatenate(
        [jnp.where(lane == base + f, total[32 * pc : 32 * pc + 32], 0.0) for pc in (0, 1) for f in (0, 1)], axis=0
    ).astype(BF16)
    total = dot(local, downst[0])

    for i, (dr, dc) in enumerate(plan.offsets[0]):
        total = total + dot(s0[1 + dr, 1 + dc : 5 + dc].reshape(128, 256), weights[0][i])
    local = total.astype(BF16)
    local = jnp.concatenate([local[:, 0:128], local[:, 128:256]], axis=0)
    spread = dot(local, basis2[...])

    for e in (0, 1):
        lhs = jnp.concatenate(
            [
                pbuf[1 + e + u, 1 + v : 9 + v].reshape(256, 128)
                for u in (-1, 0, 1)
                for v in (-1, 0, 1)
            ],
            axis=1,
        )
        near = dot(lhs, table[...])
        for b in range(8):
            p, f = b // 2, b % 2
            far = spread[128 * e + 32 * p : 128 * e + 32 * p + 32, 128 * f : 128 * f + 128]
            out[e, b] = (near[32 * b : 32 * b + 32] + far).astype(BF16)

    for valid, copies in sent:

        def finish():
            for copy in copies:
                copy.wait_send()

        finish() if valid is None else pl.when(valid)(finish)


def shards(plan, probes, leaf_basis, up_transfer, down_transfer, coupling, far_ids):
    quads, cols_dev, far_levels, top = plan.quads, plan.cols_dev, plan.far_levels, plan.top
    dma = pltpu.SemaphoreType.DMA
    near_count = 4 * (1 if quads == 1 else 3) - 1
    send_count = near_count + 12 + 4 + quads * cols_dev - 1 + 4 + 8
    scratch = [
        pltpu.VMEM((4, 10, 32, 128), BF16),
        pltpu.VMEM((3, 6, 32, 256), BF16),
        pltpu.VMEM((plan.window, 2, 32, 128), BF16),
        pltpu.VMEM((plan.window, 2, 32, 128), BF16),
        pltpu.VMEM((1 if quads == 1 else 3, 3, 32, 256), BF16),
        pltpu.VMEM((quads, cols_dev, 32, 128), BF16),
        pltpu.VMEM((9 * 128, 128), BF16),
        pltpu.VMEM((64, 128), BF16),
        pltpu.SMEM(far_ids.shape, jnp.int32),
        pltpu.VMEM((128, 256), BF16),
        pltpu.VMEM((top, 4, 64, 64), BF16),
        pltpu.VMEM((top, 4, 64, 64), BF16),
        pltpu.VMEM((top, 256, 128), BF16),
        pltpu.VMEM((top, 256, 256), BF16),
    ]
    for l in range(far_levels):
        scratch.append(pltpu.VMEM((len(plan.offsets[l]), 128 * plan.ne[l], 128 * plan.ne[l]), BF16))
    scratch += [pltpu.VMEM(coupling.shape[1:], BF16) for _ in range(far_levels)]
    for l in range(3, far_levels):
        pr, pc = plan.parents[l]
        scratch.append(pltpu.VMEM((pr + 2, pc + 2, 32, 128 * plan.ne[l]), BF16))
    scratch += [
        dma((5 + far_levels,)),
        dma((send_count,)),
        dma((3, 2, 2)),
        dma((2, 2)),
        dma((2, 2, 2)),
        dma((plan.window,)),
        dma((2, 2)),
        dma((quads, cols_dev)),
    ]
    anywhere = pl.BlockSpec(memory_space=pltpu.HBM)
    vmem = pl.BlockSpec(memory_space=pltpu.VMEM)
    operands = [
        pltpu.with_memory_space_constraint(x, pltpu.HBM)
        for x in (probes, leaf_basis.T, up_transfer, down_transfer, coupling, far_ids)
    ]
    return pl.pallas_call(
        functools.partial(kernel, plan),
        out_shape=jax.ShapeDtypeStruct(probes.shape, BF16),
        in_specs=[anywhere] * 6,
        out_specs=vmem,
        scratch_shapes=scratch,
        compiler_params=pltpu.CompilerParams(
            collective_id=0, has_side_effects=True, vmem_limit_bytes=40 * 1024 * 1024
        ),
    )(*operands)


def solution(mesh):
    in_specs = (P("gx", "gy", None, None), P(), P(), P(), P(), P())
    out_specs = P("gx", "gy", None, None)

    def run(probes, leaf_basis, up_transfer, down_transfer, coupling, far_ids):
        plan = Plan(mesh.shape["gx"], mesh.shape["gy"], coupling.shape[0])
        return jax.shard_map(
            functools.partial(shards, plan), mesh=mesh, in_specs=in_specs, out_specs=out_specs, check_vma=False
        )(probes, leaf_basis, up_transfer, down_transfer, coupling, far_ids)

    return run
```

```python
import functools

import jax
import jax.numpy as jnp
from jax import lax
from jax.experimental import pallas as pl
from jax.experimental.pallas import tpu as pltpu
from jax.sharding import PartitionSpec as P

LEAF_ROWS = 8
LEAF_COLS = 16
LENGTH_SCALE = 1.5
MESH = pl.DeviceIdType.MESH
BF16 = jnp.bfloat16
F32 = jnp.float32
AROUND = [(du, dv) for du in (-1, 0, 1) for dv in (-1, 0, 1) if (du, dv) != (0, 0)]


def slot_offsets(type_row, type_col):
    offsets = []
    for off_row in range(-2 - type_row, 4 - type_row):
        for off_col in range(-2 - type_col, 4 - type_col):
            if max(abs(off_row), abs(off_col)) > 1:
                offsets.append((off_row, off_col))
    return offsets


SLOT_OF = {
    (e, f): {offset: s for s, offset in enumerate(slot_offsets(e, f))} for e in (0, 1) for f in (0, 1)
}


class Plan:
    def __init__(self, rows_dev, cols_dev, levels):
        self.rows_dev, self.cols_dev, self.levels = rows_dev, cols_dev, levels
        self.quads = rows_dev // 4
        self.pad = 2 if self.quads == 1 else 4
        self.window = 4 + 2 * self.pad
        self.grid = [(max(1, 2 * rows_dev >> l), max(1, 8 * cols_dev >> l)) for l in range(levels)]
        self.parents = [((r + 1) // 2, (c + 1) // 2) for r, c in self.grid]
        self.ne = [2 if r > 1 else 1 for r, _ in self.grid]
        self.offsets = [
            [(dr, dc) for dr, dc in AROUND if (pr > 1 or dr == 0) and (pc > 1 or dc == 0)]
            for pr, pc in self.parents
        ]
        self.top = max(l for l in range(levels) if self.offsets[l])
        self.far_levels = self.top + 1


def dot(a, b):
    return jnp.dot(a, b, preferred_element_type=F32)


def kernel(
    plan, probes, basis, up, down, coupling, ids_hbm, out,
    pbuf, s0, l1, l1side, s2, l3, table, basisv, ids, basis2, upv, downv, updup, downst, *rest,
):
    far_levels, top = plan.far_levels, plan.top
    weights, coup, rest = rest[:far_levels], rest[far_levels : 2 * far_levels], rest[2 * far_levels :]
    tops, rest = rest[: top - 2], rest[top - 2 :]
    local_sem, send_sem, rowrecv, colrecv, cornerrecv, l1recv, siderecv, l3recv = rest
    rows_dev, cols_dev, quads, pad = plan.rows_dev, plan.cols_dev, plan.quads, plan.pad
    g = lax.axis_index("gx")
    y = lax.axis_index("gy")
    quad, member = g // 4, g % 4
    quad_steps = (0,) if quads == 1 else (-1, 0, 1)

    def inside(row, col):
        return (row >= 0) & (row < rows_dev) & (col >= 0) & (col < cols_dev)

    near_partners = [(dq, k) for dq in quad_steps for k in range(4) if (dq, k) != (0, 0)]
    far_partners = [(kq, ky) for kq in range(quads) for ky in range(cols_dev) if (kq, ky) != (0, 0)]

    def near_device(dq, k):
        return (quad + dq) * 4 + (member + k) % 4, y

    def far_device(kq, ky):
        return (quad + kq) % quads * 4 + member, (y + ky) % cols_dev

    def met(row, col):
        return (abs(row // 4 - quad) <= 1) & (col == y)

    barrier = pltpu.get_barrier_semaphore()
    expected = jnp.int32(0)
    for partner in near_partners:
        row, col = near_device(*partner)
        valid = inside(row, col)

        @pl.when(valid)
        def _():
            pl.semaphore_signal(barrier, inc=1, device_id=(row, col), device_id_type=MESH)

        expected = expected + jnp.where(valid, 1, 0)
    for partner in far_partners:
        row, col = far_device(*partner)
        valid = jnp.logical_not(met(row, col))

        @pl.when(valid)
        def _():
            pl.semaphore_signal(barrier, inc=1, device_id=(row, col), device_id_type=MESH)

        expected = expected + jnp.where(valid, 1, 0)

    fetch = [
        pltpu.make_async_copy(probes, pbuf.at[1:3, 1:9], local_sem.at[0]),
        pltpu.make_async_copy(up.at[0:top], upv, local_sem.at[1]),
        pltpu.make_async_copy(down.at[0:top], downv, local_sem.at[2]),
        pltpu.make_async_copy(basis, basisv, local_sem.at[3]),
        pltpu.make_async_copy(ids_hbm, ids, local_sem.at[4]),
    ]
    fetch_coup = [
        pltpu.make_async_copy(coupling.at[l], coup[l], local_sem.at[5 + l]) for l in range(far_levels)
    ]
    for at in (3, 0, 1, 4, 2):
        fetch[at].start()
    for copy in reversed(fetch_coup):
        copy.start()

    def clear(part):
        part[...] = jnp.zeros(part.shape, BF16)

    halo_row = {1: 0, -1: 2}
    probe_row = {1: 0, -1: 3}
    own_adjacent = {1: 2, -1: 1}
    far_half = {1: slice(0, 128), -1: slice(128, 256)}
    near_half = {1: slice(128, 256), -1: slice(0, 128)}
    probe_side = {1: slice(0, 1), -1: slice(9, 10)}
    coef_side = {1: slice(0, 1), -1: slice(5, 6)}
    own_probe_edge = {1: slice(8, 9), -1: slice(1, 2)}
    own_coef_edge = {1: slice(4, 5), -1: slice(1, 2)}
    side_of = {1: 0, -1: 1}
    signs = (1, -1)

    def row_inside(row):
        return (row >= 0) & (row < rows_dev)

    def col_inside(col):
        return (col >= 0) & (col < cols_dev)

    for d in signs:

        @pl.when(jnp.logical_not(row_inside(g - d)))
        def _():
            clear(pbuf.at[probe_row[d]])
            clear(s0.at[halo_row[d]])

        @pl.when(jnp.logical_not(col_inside(y - d)))
        def _():
            clear(pbuf.at[:, probe_side[d]])
            clear(s0.at[:, coef_side[d]])
            clear(l1side.at[:, side_of[d]])
            clear(s2.at[:, 1 - d])

    if quads == 1:
        for part in (l1, l1side):
            clear(part.at[0:pad])
            clear(part.at[pad + 4 : 2 * pad + 4])
    else:

        @pl.when(quad == 0)
        def _():
            clear(l1.at[0:4])

        @pl.when(quad == quads - 1)
        def _():
            clear(l1.at[8:12])

    for level_top in tops:
        clear(level_top)

    point_q = lax.broadcasted_iota(jnp.int32, (128, 128), 0)
    point_p = lax.broadcasted_iota(jnp.int32, (128, 128), 1)
    row_apart = (point_q // LEAF_COLS - point_p // LEAF_COLS).astype(F32)
    col_apart = (point_q % LEAF_COLS - point_p % LEAF_COLS).astype(F32)
    for i, (u, v) in enumerate([(u, v) for u in (-1, 0, 1) for v in (-1, 0, 1)]):
        dr = row_apart + float(u * LEAF_ROWS)
        dc = col_apart + float(v * LEAF_COLS)
        t = jnp.sqrt(3.0 * (dr * dr + dc * dc)) / LENGTH_SCALE
        table[128 * i : 128 * i + 128] = ((1.0 + t) * jnp.exp(-t)).astype(BF16)

    basis2[...] = jnp.zeros((128, 256), BF16)
    fetch[3].wait()
    basis2[0:64, 0:128] = basisv[...]
    basis2[64:128, 128:256] = basisv[...]

    fetch[1].wait()

    def make_updup(l):
        width = plan.ne[l] * 128
        wide = upv[l, 0 : 2 * plan.ne[l]].reshape(width, 64)
        updup[l, 0:width] = jnp.concatenate([wide, wide], axis=1)

    make_updup(0)
    fetch[0].wait()
    left_rows = jnp.concatenate(
        [
            jnp.concatenate([pbuf[1 + e, 1 + 2 * p], pbuf[1 + e, 2 + 2 * p]], axis=1)
            for e in (0, 1)
            for p in range(4)
        ],
        axis=0,
    )
    leaf = lax.dot_general(
        left_rows, basis2[...], (((1,), (1,)), ((), ())), preferred_element_type=F32
    ).astype(BF16)
    own = jnp.concatenate([leaf[0:128], leaf[128:256]], axis=1)
    s0[1, 1:5] = own.reshape(4, 32, 256)

    def halves(shape):
        return lax.broadcasted_iota(jnp.int32, shape, len(shape) - 1) // 64

    half32 = halves((32, 128))
    lifted = dot(own, updup[0, 0:256])
    own_row = pad + member
    for pc in (0, 1):
        first = lifted[64 * pc : 64 * pc + 32]
        second = lifted[64 * pc + 32 : 64 * pc + 64]
        l1[own_row, pc] = jnp.where(half32 == 0, first, second).astype(BF16)

    pl.semaphore_wait(barrier, expected)

    sent = []
    count = [0]

    def send(valid, parts):
        copies = []
        for src, dst, recv, device in parts:
            copies.append(
                pltpu.make_async_remote_copy(
                    src_ref=src, dst_ref=dst, send_sem=send_sem.at[count[0]], recv_sem=recv,
                    device_id=device, device_id_type=MESH,
                )
            )
            count[0] += 1
        sent.append((valid, copies))

        def start():
            for copy in copies:
                copy.start()

        start() if valid is None else pl.when(valid)(start)

    def receive(valid, parts):
        def wait():
            for dst, recv in parts:
                pltpu.make_async_remote_copy(
                    src_ref=dst, dst_ref=dst, send_sem=send_sem.at[0], recv_sem=recv,
                    device_id=(g, y), device_id_type=MESH,
                ).wait_recv()

        wait() if valid is None else pl.when(valid)(wait)

    def row_parts(d, piece):
        probe_cols, coef_cols = pieces[piece]
        return [
            (
                s0.at[1, coef_cols, :, far_half[d]], s0.at[halo_row[d], coef_cols, :, far_half[d]],
                rowrecv.at[piece, side_of[d], 0], (g + d, y),
            ),
            (
                pbuf.at[own_adjacent[d], probe_cols], pbuf.at[probe_row[d], probe_cols],
                rowrecv.at[piece, side_of[d], 1], (g + d, y),
            ),
        ]

    def arrivals(parts):
        return [(dst, recv) for _, dst, recv, _ in parts]

    for dq in sorted(quad_steps, key=abs):
        valid = None if dq == 0 else (quad + dq >= 0) & (quad + dq < quads)
        row = pad - 4 * dq + member
        send(valid, [
            (l1.at[own_row], l1.at[row], l1recv.at[row], near_device(q, k)) for q, k in near_partners if q == dq
        ])

    pieces = [(slice(1, 3), slice(1, 2)), (slice(7, 9), slice(4, 5)), (slice(3, 7), slice(2, 4))]
    for d in signs:
        send(row_inside(g + d), row_parts(d, 0) + row_parts(d, 1))

    def col_parts(d):
        return [
            (s0.at[1, own_coef_edge[d]], s0.at[1, coef_side[d]], colrecv.at[side_of[d], 0], (g, y + d)),
            (pbuf.at[1:3, own_probe_edge[d]], pbuf.at[1:3, probe_side[d]], colrecv.at[side_of[d], 1], (g, y + d)),
        ]


    for l in range(1, top):
        make_updup(l)

    for dq in sorted(quad_steps, key=abs):
        valid = None if dq == 0 else (quad + dq >= 0) & (quad + dq < quads)
        rows = [pad + 4 * dq + (member + k) % 4 for q, k in near_partners if q == dq]
        receive(valid, [(l1.at[row], l1recv.at[row]) for row in rows])
    parts = []
    for dq in quad_steps:
        for e in (0, 1):
            for pc in (0, 1):
                row = pad + 4 * dq + 2 * e
                parts.append(jnp.concatenate([l1[row, pc], l1[row + 1, pc]], axis=1))
    lift = dot(jnp.concatenate(parts, axis=0), updup[1, 0:256])
    for i, dq in enumerate(quad_steps):
        both = []
        for e in (0, 1):
            at = 128 * i + 64 * e
            both.append(jnp.where(half32 == 0, lift[at : at + 32], lift[at + 32 : at + 64]))
        s2[i, 1] = jnp.concatenate(both, axis=1).astype(BF16)
    lift = dot(s2[quad_steps.index(0), 1], updup[2, 0:256])
    l3[quad, y] = jnp.where(half32 == y % 2, lift, 0.0).astype(BF16)
    send(None, [
        (l3.at[quad, y], l3.at[quad, y], l3recv.at[quad, y], far_device(kq, ky)) for kq, ky in far_partners
    ])
    rows_sent = slice(pad, pad + 4) if quads == 1 else slice(0, plan.window)

    def side_parts(d):
        return [
            (l1.at[rows_sent, (1 + d) // 2], l1side.at[rows_sent, side_of[d]], siderecv.at[side_of[d], 0], (g, y + d)),
            (s2.at[:, 1], s2.at[:, 1 - d], siderecv.at[side_of[d], 1], (g, y + d)),
        ]

    for d in signs:
        send(col_inside(y + d), side_parts(d) + col_parts(d))
    for d in signs:
        send(row_inside(g + d), row_parts(d, 2))

    def adjacent(parents):
        rows = [
            jnp.concatenate([pbuf[probe_row[d], 2 * p - 1], pbuf[probe_row[d], 2 * p]], axis=1)
            for d in signs
            for p in parents
        ]
        coefs = lax.dot_general(
            jnp.concatenate(rows, axis=0), basis2[...], (((1,), (1,)), ((), ())), preferred_element_type=F32
        ).astype(BF16)
        at = 0
        for d in signs:
            for p in parents:
                s0[halo_row[d], p, :, near_half[d]] = coefs[at : at + 32]
                at += 32

    def corner_parts(d, v):
        return [
            (
                s0.at[halo_row[d], own_coef_edge[v]], s0.at[halo_row[d], coef_side[v]],
                cornerrecv.at[side_of[d], side_of[v], 0], (g, y + v),
            ),
            (
                pbuf.at[probe_row[d], own_probe_edge[v]], pbuf.at[probe_row[d], probe_side[v]],
                cornerrecv.at[side_of[d], side_of[v], 1], (g, y + v),
            ),
        ]

    for d in signs:
        receive(row_inside(g - d), arrivals(row_parts(d, 0) + row_parts(d, 1)))
    adjacent((1, 4))
    for d in signs:
        for v in signs:
            send(row_inside(g - d) & col_inside(y + v), corner_parts(d, v))

    fetch[2].wait()
    for l in range(top):
        for e in range(plan.ne[l]):
            wide = jnp.concatenate([downv[l, 2 * e], downv[l, 2 * e + 1]], axis=1)
            for c in range(2 * plan.ne[l + 1]):
                downst[l, 64 * c : 64 * c + 64, 128 * e : 128 * e + 128] = wide

    empty = jnp.zeros((64, 64), BF16)

    def assemble(l):
        fetch_coup[l].wait()
        for i, (dr, dc) in enumerate(plan.offsets[l]):
            for se in range(plan.ne[l]):
                for sf in (0, 1):
                    for e in range(plan.ne[l]):
                        pair = []
                        for f in (0, 1):
                            slot = SLOT_OF[e, f].get((2 * dr + se - e, 2 * dc + sf - f))
                            pair.append(empty if slot is None else coup[l][ids[l, 2 * e + f, slot]])
                        c = 2 * se + sf
                        weights[l][i, 64 * c : 64 * c + 64, 128 * e : 128 * e + 128] = jnp.concatenate(pair, axis=1)

    fetch[4].wait()
    for l in reversed(range(2, far_levels)):
        assemble(l)

    assemble(1)
    assemble(0)

    receive(None, [
        (l3.at[row, col], l3recv.at[row, col])
        for row, col in [((quad + kq) % quads, (y + ky) % cols_dev) for kq, ky in far_partners]
    ])
    for d in signs:
        receive(col_inside(y - d), arrivals(side_parts(d) + col_parts(d)))
    for d in signs:
        receive(row_inside(g - d), arrivals(row_parts(d, 2)))
    for d in signs:
        for v in signs:
            receive(row_inside(g - d) & col_inside(y - v), arrivals(corner_parts(d, v)))
    adjacent((2, 3))

    pair_row = pad + 2 * (member // 2)
    far1 = jnp.zeros((64, 256), F32)
    for dr in (-1, 0, 1):
        row = pair_row + 2 * dr
        tiles = [
            jnp.concatenate([ref[row, at], ref[row + 1, at]], axis=1)
            for ref, at in ((l1side, 0), (l1, 0), (l1, 1), (l1side, 1))
        ]
        for dc in (-1, 0, 1):
            if (dr, dc) in plan.offsets[1]:
                lhs = jnp.concatenate([tiles[1 + dc], tiles[2 + dc]], axis=0)
                far1 = far1 + dot(lhs, weights[1][plan.offsets[1].index((dr, dc))])
    far2 = jnp.zeros((32, 256), F32)
    for i, (dr, dc) in enumerate(plan.offsets[2]):
        far2 = far2 + dot(s2[quad_steps.index(dr), 1 + dc], weights[2][i])

    for l in range(3, far_levels):
        pr_count, pc_count = plan.parents[l]
        level_top = tops[l - 3]
        if l == 3:
            for pr in range(pr_count):
                for pc in range(pc_count):
                    for e in range(plan.ne[3]):
                        level_top[1 + pr, 1 + pc, :, 128 * e : 128 * e + 128] = (
                            l3[2 * pr + e, 2 * pc] + l3[2 * pr + e, 2 * pc + 1]
                        )
        else:
            rows_below, cols_below = plan.grid[l]
            for r in range(rows_below):
                below = tops[l - 4][1 + r, 1 : 1 + cols_below].reshape(32 * cols_below, -1)
                lift = dot(below, updup[l - 1, 0 : below.shape[1]])
                for pc in range(pc_count):
                    first, second = lift[64 * pc : 64 * pc + 32], lift[64 * pc + 32 : 64 * pc + 64]
                    e = r % 2
                    level_top[1 + r // 2, 1 + pc, :, 128 * e : 128 * e + 128] = jnp.where(
                        half32 == 0, first, second
                    ).astype(BF16)

    def far_top(l):
        width = 128 * plan.ne[l]
        pr, pc = quad >> (l - 2), y >> (l - 2)
        total = jnp.zeros((32, width), F32)
        for i, (dr, dc) in enumerate(plan.offsets[l]):
            total = total + dot(tops[l - 3][1 + pr + dr, 1 + pc + dc], weights[l][i])
        return total

    local = None
    for l in reversed(range(3, far_levels)):
        total = far_top(l)
        if local is not None:
            total = total + dot(local, downst[l, 0 : local.shape[1], 0 : total.shape[1]])
        child = 2 * ((quad >> (l - 3)) % 2) + (y >> (l - 3)) % 2
        local = jnp.where(halves(total.shape) == child, total, 0.0).astype(BF16)
    total = far2 + dot(local, downst[2, 0 : local.shape[1], 0:256])
    lane = halves(total.shape)
    base = 2 * (g // 2 % 2)
    local = jnp.concatenate([jnp.where(lane == base + f, total, 0.0) for f in (0, 1)], axis=0).astype(BF16)
    total = far1 + dot(local, downst[1])
    base = 2 * (g % 2)
    local = jnp.concatenate(
        [jnp.where(lane == base + f, total[32 * pc : 32 * pc + 32], 0.0) for pc in (0, 1) for f in (0, 1)], axis=0
    ).astype(BF16)
    total = dot(local, downst[0])

    for i, (dr, dc) in enumerate(plan.offsets[0]):
        total = total + dot(s0[1 + dr, 1 + dc : 5 + dc].reshape(128, 256), weights[0][i])
    local = total.astype(BF16)
    local = jnp.concatenate([local[:, 0:128], local[:, 128:256]], axis=0)
    spread = dot(local, basis2[...])

    for e in (0, 1):
        lhs = jnp.concatenate(
            [
                pbuf[1 + e + u, 1 + v : 9 + v].reshape(256, 128)
                for u in (-1, 0, 1)
                for v in (-1, 0, 1)
            ],
            axis=1,
        )
        near = dot(lhs, table[...])
        for b in range(8):
            p, f = b // 2, b % 2
            far = spread[128 * e + 32 * p : 128 * e + 32 * p + 32, 128 * f : 128 * f + 128]
            out[e, b] = (near[32 * b : 32 * b + 32] + far).astype(BF16)

    for valid, copies in sent:

        def finish():
            for copy in copies:
                copy.wait_send()

        finish() if valid is None else pl.when(valid)(finish)


def shards(plan, probes, leaf_basis, up_transfer, down_transfer, coupling, far_ids):
    quads, cols_dev, far_levels, top = plan.quads, plan.cols_dev, plan.far_levels, plan.top
    dma = pltpu.SemaphoreType.DMA
    near_count = 4 * (1 if quads == 1 else 3) - 1
    send_count = near_count + 12 + 4 + quads * cols_dev - 1 + 4 + 8
    scratch = [
        pltpu.VMEM((4, 10, 32, 128), BF16),
        pltpu.VMEM((3, 6, 32, 256), BF16),
        pltpu.VMEM((plan.window, 2, 32, 128), BF16),
        pltpu.VMEM((plan.window, 2, 32, 128), BF16),
        pltpu.VMEM((1 if quads == 1 else 3, 3, 32, 256), BF16),
        pltpu.VMEM((quads, cols_dev, 32, 128), BF16),
        pltpu.VMEM((9 * 128, 128), BF16),
        pltpu.VMEM((64, 128), BF16),
        pltpu.SMEM(far_ids.shape, jnp.int32),
        pltpu.VMEM((128, 256), BF16),
        pltpu.VMEM((top, 4, 64, 64), BF16),
        pltpu.VMEM((top, 4, 64, 64), BF16),
        pltpu.VMEM((top, 256, 128), BF16),
        pltpu.VMEM((top, 256, 256), BF16),
    ]
    for l in range(far_levels):
        scratch.append(pltpu.VMEM((len(plan.offsets[l]), 128 * plan.ne[l], 128 * plan.ne[l]), BF16))
    scratch += [pltpu.VMEM(coupling.shape[1:], BF16) for _ in range(far_levels)]
    for l in range(3, far_levels):
        pr, pc = plan.parents[l]
        scratch.append(pltpu.VMEM((pr + 2, pc + 2, 32, 128 * plan.ne[l]), BF16))
    scratch += [
        dma((5 + far_levels,)),
        dma((send_count,)),
        dma((3, 2, 2)),
        dma((2, 2)),
        dma((2, 2, 2)),
        dma((plan.window,)),
        dma((2, 2)),
        dma((quads, cols_dev)),
    ]
    anywhere = pl.BlockSpec(memory_space=pltpu.HBM)
    vmem = pl.BlockSpec(memory_space=pltpu.VMEM)
    operands = [
        pltpu.with_memory_space_constraint(x, pltpu.HBM)
        for x in (probes, leaf_basis.T, up_transfer, down_transfer, coupling, far_ids)
    ]
    return pl.pallas_call(
        functools.partial(kernel, plan),
        out_shape=jax.ShapeDtypeStruct(probes.shape, BF16),
        in_specs=[anywhere] * 6,
        out_specs=vmem,
        scratch_shapes=scratch,
        compiler_params=pltpu.CompilerParams(
            collective_id=0, has_side_effects=True, vmem_limit_bytes=40 * 1024 * 1024
        ),
    )(*operands)


def solution(mesh):
    in_specs = (P("gx", "gy", None, None), P(), P(), P(), P(), P())
    out_specs = P("gx", "gy", None, None)

    def run(probes, leaf_basis, up_transfer, down_transfer, coupling, far_ids):
        plan = Plan(mesh.shape["gx"], mesh.shape["gy"], coupling.shape[0])
        return jax.shard_map(
            functools.partial(shards, plan), mesh=mesh, in_specs=in_specs, out_specs=out_specs, check_vma=False
        )(probes, leaf_basis, up_transfer, down_transfer, coupling, far_ids)

    return run
```

```python
import functools

import jax
import jax.numpy as jnp
from jax import lax
from jax.experimental import pallas as pl
from jax.experimental.pallas import tpu as pltpu
from jax.sharding import PartitionSpec as P

LEAF_ROWS = 8
LEAF_COLS = 16
LENGTH_SCALE = 1.5
MESH = pl.DeviceIdType.MESH
BF16 = jnp.bfloat16
F32 = jnp.float32
AROUND = [(du, dv) for du in (-1, 0, 1) for dv in (-1, 0, 1) if (du, dv) != (0, 0)]


def slot_offsets(type_row, type_col):
    offsets = []
    for off_row in range(-2 - type_row, 4 - type_row):
        for off_col in range(-2 - type_col, 4 - type_col):
            if max(abs(off_row), abs(off_col)) > 1:
                offsets.append((off_row, off_col))
    return offsets


SLOT_OF = {
    (e, f): {offset: s for s, offset in enumerate(slot_offsets(e, f))} for e in (0, 1) for f in (0, 1)
}


class Plan:
    def __init__(self, rows_dev, cols_dev, levels):
        self.rows_dev, self.cols_dev, self.levels = rows_dev, cols_dev, levels
        self.quads = rows_dev // 4
        self.pad = 2 if self.quads == 1 else 4
        self.window = 4 + 2 * self.pad
        self.grid = [(max(1, 2 * rows_dev >> l), max(1, 8 * cols_dev >> l)) for l in range(levels)]
        self.parents = [((r + 1) // 2, (c + 1) // 2) for r, c in self.grid]
        self.ne = [2 if r > 1 else 1 for r, _ in self.grid]
        self.offsets = [
            [(dr, dc) for dr, dc in AROUND if (pr > 1 or dr == 0) and (pc > 1 or dc == 0)]
            for pr, pc in self.parents
        ]
        self.top = max(l for l in range(levels) if self.offsets[l])
        self.far_levels = self.top + 1


def dot(a, b):
    return jnp.dot(a, b, preferred_element_type=F32)


def kernel(
    plan, probes, basis, up, down, coupling, ids_hbm, out,
    pbuf, s0, l1, l1side, s2, l3, table, basisv, ids, basis2, upv, downv, updup, downst, *rest,
):
    far_levels, top = plan.far_levels, plan.top
    weights, coup, rest = rest[:far_levels], rest[far_levels : 2 * far_levels], rest[2 * far_levels :]
    tops, rest = rest[: top - 2], rest[top - 2 :]
    local_sem, send_sem, rowrecv, colrecv, cornerrecv, l1recv, siderecv, l3recv = rest
    rows_dev, cols_dev, quads, pad = plan.rows_dev, plan.cols_dev, plan.quads, plan.pad
    g = lax.axis_index("gx")
    y = lax.axis_index("gy")
    quad, member = g // 4, g % 4
    quad_steps = (0,) if quads == 1 else (-1, 0, 1)

    def inside(row, col):
        return (row >= 0) & (row < rows_dev) & (col >= 0) & (col < cols_dev)

    near_partners = [(dq, k) for dq in quad_steps for k in range(4) if (dq, k) != (0, 0)]
    far_partners = [(kq, ky) for kq in range(quads) for ky in range(cols_dev) if (kq, ky) != (0, 0)]

    def near_device(dq, k):
        return (quad + dq) * 4 + (member + k) % 4, y

    def far_device(kq, ky):
        return (quad + kq) % quads * 4 + member, (y + ky) % cols_dev

    def met(row, col):
        return (abs(row // 4 - quad) <= 1) & (col == y)

    barrier = pltpu.get_barrier_semaphore()
    expected = jnp.int32(0)
    for partner in near_partners:
        row, col = near_device(*partner)
        valid = inside(row, col)

        @pl.when(valid)
        def _():
            pl.semaphore_signal(barrier, inc=1, device_id=(row, col), device_id_type=MESH)

        expected = expected + jnp.where(valid, 1, 0)
    for partner in far_partners:
        row, col = far_device(*partner)
        valid = jnp.logical_not(met(row, col))

        @pl.when(valid)
        def _():
            pl.semaphore_signal(barrier, inc=1, device_id=(row, col), device_id_type=MESH)

        expected = expected + jnp.where(valid, 1, 0)

    fetch = [
        pltpu.make_async_copy(probes, pbuf.at[1:3, 1:9], local_sem.at[0]),
        pltpu.make_async_copy(up.at[0:top], upv, local_sem.at[1]),
        pltpu.make_async_copy(down.at[0:top], downv, local_sem.at[2]),
        pltpu.make_async_copy(basis, basisv, local_sem.at[3]),
        pltpu.make_async_copy(ids_hbm, ids, local_sem.at[4]),
    ]
    fetch_coup = [
        pltpu.make_async_copy(coupling.at[l], coup[l], local_sem.at[5 + l]) for l in range(far_levels)
    ]
    for at in (3, 0, 1, 4, 2):
        fetch[at].start()
    for copy in reversed(fetch_coup):
        copy.start()

    def clear(part):
        part[...] = jnp.zeros(part.shape, BF16)

    halo_row = {1: 0, -1: 2}
    probe_row = {1: 0, -1: 3}
    own_adjacent = {1: 2, -1: 1}
    far_half = {1: slice(0, 128), -1: slice(128, 256)}
    near_half = {1: slice(128, 256), -1: slice(0, 128)}
    probe_side = {1: slice(0, 1), -1: slice(9, 10)}
    coef_side = {1: slice(0, 1), -1: slice(5, 6)}
    own_probe_edge = {1: slice(8, 9), -1: slice(1, 2)}
    own_coef_edge = {1: slice(4, 5), -1: slice(1, 2)}
    side_of = {1: 0, -1: 1}
    signs = (1, -1)

    def row_inside(row):
        return (row >= 0) & (row < rows_dev)

    def col_inside(col):
        return (col >= 0) & (col < cols_dev)

    for d in signs:

        @pl.when(jnp.logical_not(row_inside(g - d)))
        def _():
            clear(pbuf.at[probe_row[d]])
            clear(s0.at[halo_row[d]])

        @pl.when(jnp.logical_not(col_inside(y - d)))
        def _():
            clear(pbuf.at[:, probe_side[d]])
            clear(s0.at[:, coef_side[d]])
            clear(l1side.at[:, side_of[d]])
            clear(s2.at[:, 1 - d])

    if quads == 1:
        for part in (l1, l1side):
            clear(part.at[0:pad])
            clear(part.at[pad + 4 : 2 * pad + 4])
    else:

        @pl.when(quad == 0)
        def _():
            clear(l1.at[0:4])

        @pl.when(quad == quads - 1)
        def _():
            clear(l1.at[8:12])

    for level_top in tops:
        clear(level_top)

    point_q = lax.broadcasted_iota(jnp.int32, (128, 128), 0)
    point_p = lax.broadcasted_iota(jnp.int32, (128, 128), 1)
    row_apart = (point_q // LEAF_COLS - point_p // LEAF_COLS).astype(F32)
    col_apart = (point_q % LEAF_COLS - point_p % LEAF_COLS).astype(F32)
    for i, (u, v) in enumerate([(u, v) for u in (-1, 0, 1) for v in (-1, 0, 1)]):
        dr = row_apart + float(u * LEAF_ROWS)
        dc = col_apart + float(v * LEAF_COLS)
        t = jnp.sqrt(3.0 * (dr * dr + dc * dc)) / LENGTH_SCALE
        table[128 * i : 128 * i + 128] = ((1.0 + t) * jnp.exp(-t)).astype(BF16)

    basis2[...] = jnp.zeros((128, 256), BF16)
    fetch[3].wait()
    basis2[0:64, 0:128] = basisv[...]
    basis2[64:128, 128:256] = basisv[...]

    fetch[1].wait()

    def make_updup(l):
        width = plan.ne[l] * 128
        wide = upv[l, 0 : 2 * plan.ne[l]].reshape(width, 64)
        updup[l, 0:width] = jnp.concatenate([wide, wide], axis=1)

    make_updup(0)
    fetch[0].wait()
    left_rows = jnp.concatenate(
        [
            jnp.concatenate([pbuf[1 + e, 1 + 2 * p], pbuf[1 + e, 2 + 2 * p]], axis=1)
            for e in (0, 1)
            for p in range(4)
        ],
        axis=0,
    )
    leaf = lax.dot_general(
        left_rows, basis2[...], (((1,), (1,)), ((), ())), preferred_element_type=F32
    ).astype(BF16)
    own = jnp.concatenate([leaf[0:128], leaf[128:256]], axis=1)
    s0[1, 1:5] = own.reshape(4, 32, 256)

    def halves(shape):
        return lax.broadcasted_iota(jnp.int32, shape, len(shape) - 1) // 64

    half32 = halves((32, 128))
    lifted = dot(own, updup[0, 0:256])
    own_row = pad + member
    for pc in (0, 1):
        first = lifted[64 * pc : 64 * pc + 32]
        second = lifted[64 * pc + 32 : 64 * pc + 64]
        l1[own_row, pc] = jnp.where(half32 == 0, first, second).astype(BF16)

    pl.semaphore_wait(barrier, expected)

    sent = []
    count = [0]

    def send(valid, parts):
        copies = []
        for src, dst, recv, device in parts:
            copies.append(
                pltpu.make_async_remote_copy(
                    src_ref=src, dst_ref=dst, send_sem=send_sem.at[count[0]], recv_sem=recv,
                    device_id=device, device_id_type=MESH,
                )
            )
            count[0] += 1
        sent.append((valid, copies))

        def start():
            for copy in copies:
                copy.start()

        start() if valid is None else pl.when(valid)(start)

    def receive(valid, parts):
        def wait():
            for dst, recv in parts:
                pltpu.make_async_remote_copy(
                    src_ref=dst, dst_ref=dst, send_sem=send_sem.at[0], recv_sem=recv,
                    device_id=(g, y), device_id_type=MESH,
                ).wait_recv()

        wait() if valid is None else pl.when(valid)(wait)

    def row_parts(d, piece):
        probe_cols, coef_cols = pieces[piece]
        return [
            (
                s0.at[1, coef_cols, :, far_half[d]], s0.at[halo_row[d], coef_cols, :, far_half[d]],
                rowrecv.at[piece, side_of[d], 0], (g + d, y),
            ),
            (
                pbuf.at[own_adjacent[d], probe_cols], pbuf.at[probe_row[d], probe_cols],
                rowrecv.at[piece, side_of[d], 1], (g + d, y),
            ),
        ]

    def arrivals(parts):
        return [(dst, recv) for _, dst, recv, _ in parts]

    for dq in sorted(quad_steps, key=abs):
        valid = None if dq == 0 else (quad + dq >= 0) & (quad + dq < quads)
        row = pad - 4 * dq + member
        send(valid, [
            (l1.at[own_row], l1.at[row], l1recv.at[row], near_device(q, k)) for q, k in near_partners if q == dq
        ])

    pieces = [(slice(1, 3), slice(1, 2)), (slice(7, 9), slice(4, 5)), (slice(3, 7), slice(2, 4))]
    for d in signs:
        send(row_inside(g + d), row_parts(d, 0) + row_parts(d, 1))

    def col_parts(d):
        return [
            (s0.at[1, own_coef_edge[d]], s0.at[1, coef_side[d]], colrecv.at[side_of[d], 0], (g, y + d)),
            (pbuf.at[1:3, own_probe_edge[d]], pbuf.at[1:3, probe_side[d]], colrecv.at[side_of[d], 1], (g, y + d)),
        ]

    for d in signs:
        send(row_inside(g + d), row_parts(d, 2))
    for d in signs:
        send(col_inside(y + d), col_parts(d))

    for l in range(1, top):
        make_updup(l)

    fetch[2].wait()
    for l in range(top):
        for e in range(plan.ne[l]):
            wide = jnp.concatenate([downv[l, 2 * e], downv[l, 2 * e + 1]], axis=1)
            for c in range(2 * plan.ne[l + 1]):
                downst[l, 64 * c : 64 * c + 64, 128 * e : 128 * e + 128] = wide

    empty = jnp.zeros((64, 64), BF16)

    def assemble(l):
        fetch_coup[l].wait()
        for i, (dr, dc) in enumerate(plan.offsets[l]):
            for se in range(plan.ne[l]):
                for sf in (0, 1):
                    for e in range(plan.ne[l]):
                        pair = []
                        for f in (0, 1):
                            slot = SLOT_OF[e, f].get((2 * dr + se - e, 2 * dc + sf - f))
                            pair.append(empty if slot is None else coup[l][ids[l, 2 * e + f, slot]])
                        c = 2 * se + sf
                        weights[l][i, 64 * c : 64 * c + 64, 128 * e : 128 * e + 128] = jnp.concatenate(pair, axis=1)

    fetch[4].wait()
    for l in reversed(range(2, far_levels)):
        assemble(l)

    for dq in sorted(quad_steps, key=abs):
        valid = None if dq == 0 else (quad + dq >= 0) & (quad + dq < quads)
        rows = [pad + 4 * dq + (member + k) % 4 for q, k in near_partners if q == dq]
        receive(valid, [(l1.at[row], l1recv.at[row]) for row in rows])
    parts = []
    for dq in quad_steps:
        for e in (0, 1):
            for pc in (0, 1):
                row = pad + 4 * dq + 2 * e
                parts.append(jnp.concatenate([l1[row, pc], l1[row + 1, pc]], axis=1))
    lift = dot(jnp.concatenate(parts, axis=0), updup[1, 0:256])
    for i, dq in enumerate(quad_steps):
        both = []
        for e in (0, 1):
            at = 128 * i + 64 * e
            both.append(jnp.where(half32 == 0, lift[at : at + 32], lift[at + 32 : at + 64]))
        s2[i, 1] = jnp.concatenate(both, axis=1).astype(BF16)
    lift = dot(s2[quad_steps.index(0), 1], updup[2, 0:256])
    l3[quad, y] = jnp.where(half32 == y % 2, lift, 0.0).astype(BF16)
    send(None, [
        (l3.at[quad, y], l3.at[quad, y], l3recv.at[quad, y], far_device(kq, ky)) for kq, ky in far_partners
    ])
    rows_sent = slice(pad, pad + 4) if quads == 1 else slice(0, plan.window)

    def side_parts(d):
        return [
            (l1.at[rows_sent, (1 + d) // 2], l1side.at[rows_sent, side_of[d]], siderecv.at[side_of[d], 0], (g, y + d)),
            (s2.at[:, 1], s2.at[:, 1 - d], siderecv.at[side_of[d], 1], (g, y + d)),
        ]

    for d in signs:
        send(col_inside(y + d), side_parts(d))

    def adjacent(parents):
        rows = [
            jnp.concatenate([pbuf[probe_row[d], 2 * p - 1], pbuf[probe_row[d], 2 * p]], axis=1)
            for d in signs
            for p in parents
        ]
        coefs = lax.dot_general(
            jnp.concatenate(rows, axis=0), basis2[...], (((1,), (1,)), ((), ())), preferred_element_type=F32
        ).astype(BF16)
        at = 0
        for d in signs:
            for p in parents:
                s0[halo_row[d], p, :, near_half[d]] = coefs[at : at + 32]
                at += 32

    def corner_parts(d, v):
        return [
            (
                s0.at[halo_row[d], own_coef_edge[v]], s0.at[halo_row[d], coef_side[v]],
                cornerrecv.at[side_of[d], side_of[v], 0], (g, y + v),
            ),
            (
                pbuf.at[probe_row[d], own_probe_edge[v]], pbuf.at[probe_row[d], probe_side[v]],
                cornerrecv.at[side_of[d], side_of[v], 1], (g, y + v),
            ),
        ]

    for d in signs:
        receive(row_inside(g - d), arrivals(row_parts(d, 0) + row_parts(d, 1)))
    adjacent((1, 4))
    for d in signs:
        for v in signs:
            send(row_inside(g - d) & col_inside(y + v), corner_parts(d, v))

    assemble(1)
    assemble(0)

    receive(None, [
        (l3.at[row, col], l3recv.at[row, col])
        for row, col in [((quad + kq) % quads, (y + ky) % cols_dev) for kq, ky in far_partners]
    ])
    for d in signs:
        receive(col_inside(y - d), arrivals(side_parts(d) + col_parts(d)))

    pair_row = pad + 2 * (member // 2)
    far1 = jnp.zeros((64, 256), F32)
    for dr in (-1, 0, 1):
        row = pair_row + 2 * dr
        tiles = [
            jnp.concatenate([ref[row, at], ref[row + 1, at]], axis=1)
            for ref, at in ((l1side, 0), (l1, 0), (l1, 1), (l1side, 1))
        ]
        for dc in (-1, 0, 1):
            if (dr, dc) in plan.offsets[1]:
                lhs = jnp.concatenate([tiles[1 + dc], tiles[2 + dc]], axis=0)
                far1 = far1 + dot(lhs, weights[1][plan.offsets[1].index((dr, dc))])
    far2 = jnp.zeros((32, 256), F32)
    for i, (dr, dc) in enumerate(plan.offsets[2]):
        far2 = far2 + dot(s2[quad_steps.index(dr), 1 + dc], weights[2][i])

    for l in range(3, far_levels):
        pr_count, pc_count = plan.parents[l]
        level_top = tops[l - 3]
        if l == 3:
            for pr in range(pr_count):
                for pc in range(pc_count):
                    for e in range(plan.ne[3]):
                        level_top[1 + pr, 1 + pc, :, 128 * e : 128 * e + 128] = (
                            l3[2 * pr + e, 2 * pc] + l3[2 * pr + e, 2 * pc + 1]
                        )
        else:
            rows_below, cols_below = plan.grid[l]
            for r in range(rows_below):
                below = tops[l - 4][1 + r, 1 : 1 + cols_below].reshape(32 * cols_below, -1)
                lift = dot(below, updup[l - 1, 0 : below.shape[1]])
                for pc in range(pc_count):
                    first, second = lift[64 * pc : 64 * pc + 32], lift[64 * pc + 32 : 64 * pc + 64]
                    e = r % 2
                    level_top[1 + r // 2, 1 + pc, :, 128 * e : 128 * e + 128] = jnp.where(
                        half32 == 0, first, second
                    ).astype(BF16)

    def far_top(l):
        width = 128 * plan.ne[l]
        pr, pc = quad >> (l - 2), y >> (l - 2)
        total = jnp.zeros((32, width), F32)
        for i, (dr, dc) in enumerate(plan.offsets[l]):
            total = total + dot(tops[l - 3][1 + pr + dr, 1 + pc + dc], weights[l][i])
        return total

    local = None
    for l in reversed(range(3, far_levels)):
        total = far_top(l)
        if local is not None:
            total = total + dot(local, downst[l, 0 : local.shape[1], 0 : total.shape[1]])
        child = 2 * ((quad >> (l - 3)) % 2) + (y >> (l - 3)) % 2
        local = jnp.where(halves(total.shape) == child, total, 0.0).astype(BF16)
    total = far2 + dot(local, downst[2, 0 : local.shape[1], 0:256])
    lane = halves(total.shape)
    base = 2 * (g // 2 % 2)
    local = jnp.concatenate([jnp.where(lane == base + f, total, 0.0) for f in (0, 1)], axis=0).astype(BF16)
    total = far1 + dot(local, downst[1])
    base = 2 * (g % 2)
    local = jnp.concatenate(
        [jnp.where(lane == base + f, total[32 * pc : 32 * pc + 32], 0.0) for pc in (0, 1) for f in (0, 1)], axis=0
    ).astype(BF16)
    total = dot(local, downst[0])

    def far_leaf(total, rows):
        for i, (dr, dc) in enumerate(plan.offsets[0]):
            if dr in rows:
                total = total + dot(s0[1 + dr, 1 + dc : 5 + dc].reshape(128, 256), weights[0][i])
        return total

    def near_rows(e, offs):
        lhs = jnp.concatenate(
            [pbuf[1 + e + u, 1 + v : 9 + v].reshape(256, 128) for u in offs for v in (-1, 0, 1)], axis=1
        )
        first = 384 * (offs[0] + 1)
        return dot(lhs, table[first : first + 384 * len(offs)])

    total = far_leaf(total, (0,))
    near_own = [near_rows(e, (-e, 1 - e)) for e in (0, 1)]

    for d in signs:
        receive(row_inside(g - d), arrivals(row_parts(d, 2)))
    for d in signs:
        for v in signs:
            receive(row_inside(g - d) & col_inside(y - v), arrivals(corner_parts(d, v)))
    adjacent((2, 3))
    total = far_leaf(total, (-1, 1))
    local = total.astype(BF16)
    local = jnp.concatenate([local[:, 0:128], local[:, 128:256]], axis=0)
    spread = dot(local, basis2[...])
    for e in (0, 1):
        near = near_own[e] + near_rows(e, (2 * e - 1,))
        for b in range(8):
            p, f = b // 2, b % 2
            far = spread[128 * e + 32 * p : 128 * e + 32 * p + 32, 128 * f : 128 * f + 128]
            out[e, b] = (near[32 * b : 32 * b + 32] + far).astype(BF16)

    for valid, copies in sent:

        def finish():
            for copy in copies:
                copy.wait_send()

        finish() if valid is None else pl.when(valid)(finish)


def shards(plan, probes, leaf_basis, up_transfer, down_transfer, coupling, far_ids):
    quads, cols_dev, far_levels, top = plan.quads, plan.cols_dev, plan.far_levels, plan.top
    dma = pltpu.SemaphoreType.DMA
    near_count = 4 * (1 if quads == 1 else 3) - 1
    send_count = near_count + 12 + 4 + quads * cols_dev - 1 + 4 + 8
    scratch = [
        pltpu.VMEM((4, 10, 32, 128), BF16),
        pltpu.VMEM((3, 6, 32, 256), BF16),
        pltpu.VMEM((plan.window, 2, 32, 128), BF16),
        pltpu.VMEM((plan.window, 2, 32, 128), BF16),
        pltpu.VMEM((1 if quads == 1 else 3, 3, 32, 256), BF16),
        pltpu.VMEM((quads, cols_dev, 32, 128), BF16),
        pltpu.VMEM((9 * 128, 128), BF16),
        pltpu.VMEM((64, 128), BF16),
        pltpu.SMEM(far_ids.shape, jnp.int32),
        pltpu.VMEM((128, 256), BF16),
        pltpu.VMEM((top, 4, 64, 64), BF16),
        pltpu.VMEM((top, 4, 64, 64), BF16),
        pltpu.VMEM((top, 256, 128), BF16),
        pltpu.VMEM((top, 256, 256), BF16),
    ]
    for l in range(far_levels):
        scratch.append(pltpu.VMEM((len(plan.offsets[l]), 128 * plan.ne[l], 128 * plan.ne[l]), BF16))
    scratch += [pltpu.VMEM(coupling.shape[1:], BF16) for _ in range(far_levels)]
    for l in range(3, far_levels):
        pr, pc = plan.parents[l]
        scratch.append(pltpu.VMEM((pr + 2, pc + 2, 32, 128 * plan.ne[l]), BF16))
    scratch += [
        dma((5 + far_levels,)),
        dma((send_count,)),
        dma((3, 2, 2)),
        dma((2, 2)),
        dma((2, 2, 2)),
        dma((plan.window,)),
        dma((2, 2)),
        dma((quads, cols_dev)),
    ]
    anywhere = pl.BlockSpec(memory_space=pltpu.HBM)
    vmem = pl.BlockSpec(memory_space=pltpu.VMEM)
    operands = [
        pltpu.with_memory_space_constraint(x, pltpu.HBM)
        for x in (probes, leaf_basis.T, up_transfer, down_transfer, coupling, far_ids)
    ]
    return pl.pallas_call(
        functools.partial(kernel, plan),
        out_shape=jax.ShapeDtypeStruct(probes.shape, BF16),
        in_specs=[anywhere] * 6,
        out_specs=vmem,
        scratch_shapes=scratch,
        compiler_params=pltpu.CompilerParams(
            collective_id=0, has_side_effects=True, vmem_limit_bytes=40 * 1024 * 1024
        ),
    )(*operands)


def solution(mesh):
    in_specs = (P("gx", "gy", None, None), P(), P(), P(), P(), P())
    out_specs = P("gx", "gy", None, None)

    def run(probes, leaf_basis, up_transfer, down_transfer, coupling, far_ids):
        plan = Plan(mesh.shape["gx"], mesh.shape["gy"], coupling.shape[0])
        return jax.shard_map(
            functools.partial(shards, plan), mesh=mesh, in_specs=in_specs, out_specs=out_specs, check_vma=False
        )(probes, leaf_basis, up_transfer, down_transfer, coupling, far_ids)

    return run
```

```python
import functools

import jax
import jax.numpy as jnp
from jax import lax
from jax.experimental import pallas as pl
from jax.experimental.pallas import tpu as pltpu
from jax.sharding import PartitionSpec as P

LEAF_ROWS = 8
LEAF_COLS = 16
LENGTH_SCALE = 1.5
MESH = pl.DeviceIdType.MESH
BF16 = jnp.bfloat16
F32 = jnp.float32
AROUND = [(du, dv) for du in (-1, 0, 1) for dv in (-1, 0, 1) if (du, dv) != (0, 0)]


def slot_offsets(type_row, type_col):
    offsets = []
    for off_row in range(-2 - type_row, 4 - type_row):
        for off_col in range(-2 - type_col, 4 - type_col):
            if max(abs(off_row), abs(off_col)) > 1:
                offsets.append((off_row, off_col))
    return offsets


SLOT_OF = {
    (e, f): {offset: s for s, offset in enumerate(slot_offsets(e, f))} for e in (0, 1) for f in (0, 1)
}


class Plan:
    def __init__(self, rows_dev, cols_dev, levels):
        self.rows_dev, self.cols_dev, self.levels = rows_dev, cols_dev, levels
        self.quads = rows_dev // 4
        self.pad = 2 if self.quads == 1 else 4
        self.window = 4 + 2 * self.pad
        self.grid = [(max(1, 2 * rows_dev >> l), max(1, 8 * cols_dev >> l)) for l in range(levels)]
        self.parents = [((r + 1) // 2, (c + 1) // 2) for r, c in self.grid]
        self.ne = [2 if r > 1 else 1 for r, _ in self.grid]
        self.offsets = [
            [(dr, dc) for dr, dc in AROUND if (pr > 1 or dr == 0) and (pc > 1 or dc == 0)]
            for pr, pc in self.parents
        ]
        self.top = max(l for l in range(levels) if self.offsets[l])
        self.far_levels = self.top + 1


def dot(a, b):
    return jnp.dot(a, b, preferred_element_type=F32)


def kernel(
    plan, probes, basis, up, down, coupling, ids_hbm, out,
    pbuf, s0, l1, l1side, s2, l3, table, basisv, ids, basis2, upv, downv, updup, downst, *rest,
):
    far_levels, top = plan.far_levels, plan.top
    weights, coup, rest = rest[:far_levels], rest[far_levels : 2 * far_levels], rest[2 * far_levels :]
    tops, rest = rest[: top - 2], rest[top - 2 :]
    local_sem, send_sem, rowrecv, colrecv, cornerrecv, l1recv, siderecv, l3recv = rest
    rows_dev, cols_dev, quads, pad = plan.rows_dev, plan.cols_dev, plan.quads, plan.pad
    g = lax.axis_index("gx")
    y = lax.axis_index("gy")
    quad, member = g // 4, g % 4
    quad_steps = (0,) if quads == 1 else (-1, 0, 1)

    def inside(row, col):
        return (row >= 0) & (row < rows_dev) & (col >= 0) & (col < cols_dev)

    near_partners = [(dq, k) for dq in quad_steps for k in range(4) if (dq, k) != (0, 0)]
    far_partners = [(kq, ky) for kq in range(quads) for ky in range(cols_dev) if (kq, ky) != (0, 0)]

    def near_device(dq, k):
        return (quad + dq) * 4 + (member + k) % 4, y

    def far_device(kq, ky):
        return (quad + kq) % quads * 4 + member, (y + ky) % cols_dev

    def met(row, col):
        return (abs(row // 4 - quad) <= 1) & (col == y)

    barrier = pltpu.get_barrier_semaphore()
    expected = jnp.int32(0)
    for partner in near_partners:
        row, col = near_device(*partner)
        valid = inside(row, col)

        @pl.when(valid)
        def _():
            pl.semaphore_signal(barrier, inc=1, device_id=(row, col), device_id_type=MESH)

        expected = expected + jnp.where(valid, 1, 0)
    for partner in far_partners:
        row, col = far_device(*partner)
        valid = jnp.logical_not(met(row, col))

        @pl.when(valid)
        def _():
            pl.semaphore_signal(barrier, inc=1, device_id=(row, col), device_id_type=MESH)

        expected = expected + jnp.where(valid, 1, 0)

    fetch = [
        pltpu.make_async_copy(probes, pbuf.at[1:3, 1:9], local_sem.at[0]),
        pltpu.make_async_copy(up.at[0:top], upv, local_sem.at[1]),
        pltpu.make_async_copy(down.at[0:top], downv, local_sem.at[2]),
        pltpu.make_async_copy(basis, basisv, local_sem.at[3]),
        pltpu.make_async_copy(ids_hbm, ids, local_sem.at[4]),
    ]
    fetch_coup = [
        pltpu.make_async_copy(coupling.at[l], coup[l], local_sem.at[5 + l]) for l in range(far_levels)
    ]
    for at in (3, 0, 1, 4, 2):
        fetch[at].start()

    def clear(part):
        part[...] = jnp.zeros(part.shape, BF16)

    halo_row = {1: 0, -1: 2}
    probe_row = {1: 0, -1: 3}
    own_adjacent = {1: 2, -1: 1}
    far_half = {1: slice(0, 128), -1: slice(128, 256)}
    near_half = {1: slice(128, 256), -1: slice(0, 128)}
    probe_side = {1: slice(0, 1), -1: slice(9, 10)}
    coef_side = {1: slice(0, 1), -1: slice(5, 6)}
    own_probe_edge = {1: slice(8, 9), -1: slice(1, 2)}
    own_coef_edge = {1: slice(4, 5), -1: slice(1, 2)}
    side_of = {1: 0, -1: 1}
    signs = (1, -1)

    def row_inside(row):
        return (row >= 0) & (row < rows_dev)

    def col_inside(col):
        return (col >= 0) & (col < cols_dev)

    for d in signs:

        @pl.when(jnp.logical_not(row_inside(g - d)))
        def _():
            clear(pbuf.at[probe_row[d]])
            clear(s0.at[halo_row[d]])

        @pl.when(jnp.logical_not(col_inside(y - d)))
        def _():
            clear(pbuf.at[:, probe_side[d]])
            clear(s0.at[:, coef_side[d]])
            clear(l1side.at[:, side_of[d]])
            clear(s2.at[:, 1 - d])

    if quads == 1:
        for part in (l1, l1side):
            clear(part.at[0:pad])
            clear(part.at[pad + 4 : 2 * pad + 4])
    else:

        @pl.when(quad == 0)
        def _():
            clear(l1.at[0:4])

        @pl.when(quad == quads - 1)
        def _():
            clear(l1.at[8:12])

    for level_top in tops:
        clear(level_top)

    basis2[...] = jnp.zeros((128, 256), BF16)
    fetch[3].wait()
    basis2[0:64, 0:128] = basisv[...]
    basis2[64:128, 128:256] = basisv[...]

    fetch[1].wait()

    def make_updup(l):
        width = plan.ne[l] * 128
        wide = upv[l, 0 : 2 * plan.ne[l]].reshape(width, 64)
        updup[l, 0:width] = jnp.concatenate([wide, wide], axis=1)

    make_updup(0)
    fetch[0].wait()
    left_rows = jnp.concatenate(
        [
            jnp.concatenate([pbuf[1 + e, 1 + 2 * p], pbuf[1 + e, 2 + 2 * p]], axis=1)
            for e in (0, 1)
            for p in range(4)
        ],
        axis=0,
    )
    leaf = lax.dot_general(
        left_rows, basis2[...], (((1,), (1,)), ((), ())), preferred_element_type=F32
    ).astype(BF16)
    own = jnp.concatenate([leaf[0:128], leaf[128:256]], axis=1)
    s0[1, 1:5] = own.reshape(4, 32, 256)

    def halves(shape):
        return lax.broadcasted_iota(jnp.int32, shape, len(shape) - 1) // 64

    half32 = halves((32, 128))
    lifted = dot(own, updup[0, 0:256])
    own_row = pad + member
    for pc in (0, 1):
        first = lifted[64 * pc : 64 * pc + 32]
        second = lifted[64 * pc + 32 : 64 * pc + 64]
        l1[own_row, pc] = jnp.where(half32 == 0, first, second).astype(BF16)

    pl.semaphore_wait(barrier, expected)

    sent = []
    count = [0]

    def send(valid, parts):
        copies = []
        for src, dst, recv, device in parts:
            copies.append(
                pltpu.make_async_remote_copy(
                    src_ref=src, dst_ref=dst, send_sem=send_sem.at[count[0]], recv_sem=recv,
                    device_id=device, device_id_type=MESH,
                )
            )
            count[0] += 1
        sent.append((valid, copies))

        def start():
            for copy in copies:
                copy.start()

        start() if valid is None else pl.when(valid)(start)

    def receive(valid, parts):
        def wait():
            for dst, recv in parts:
                pltpu.make_async_remote_copy(
                    src_ref=dst, dst_ref=dst, send_sem=send_sem.at[0], recv_sem=recv,
                    device_id=(g, y), device_id_type=MESH,
                ).wait_recv()

        wait() if valid is None else pl.when(valid)(wait)

    def row_parts(d, piece):
        probe_cols, coef_cols = pieces[piece]
        return [
            (
                s0.at[1, coef_cols, :, far_half[d]], s0.at[halo_row[d], coef_cols, :, far_half[d]],
                rowrecv.at[piece, side_of[d], 0], (g + d, y),
            ),
            (
                pbuf.at[own_adjacent[d], probe_cols], pbuf.at[probe_row[d], probe_cols],
                rowrecv.at[piece, side_of[d], 1], (g + d, y),
            ),
        ]

    def arrivals(parts):
        return [(dst, recv) for _, dst, recv, _ in parts]

    for dq in sorted(quad_steps, key=abs):
        valid = None if dq == 0 else (quad + dq >= 0) & (quad + dq < quads)
        row = pad - 4 * dq + member
        send(valid, [
            (l1.at[own_row], l1.at[row], l1recv.at[row], near_device(q, k)) for q, k in near_partners if q == dq
        ])

    pieces = [(slice(1, 3), slice(1, 2)), (slice(7, 9), slice(4, 5)), (slice(3, 7), slice(2, 4))]
    for d in signs:
        send(row_inside(g + d), row_parts(d, 0) + row_parts(d, 1))

    def col_parts(d):
        return [
            (s0.at[1, own_coef_edge[d]], s0.at[1, coef_side[d]], colrecv.at[side_of[d], 0], (g, y + d)),
            (pbuf.at[1:3, own_probe_edge[d]], pbuf.at[1:3, probe_side[d]], colrecv.at[side_of[d], 1], (g, y + d)),
        ]

    for d in signs:
        send(row_inside(g + d), row_parts(d, 2))
    for copy in reversed(fetch_coup):
        copy.start()
    for d in signs:
        send(col_inside(y + d), col_parts(d))

    for l in range(1, top):
        make_updup(l)

    point_q = lax.broadcasted_iota(jnp.int32, (128, 128), 0)
    point_p = lax.broadcasted_iota(jnp.int32, (128, 128), 1)
    row_apart = (point_q // LEAF_COLS - point_p // LEAF_COLS).astype(F32)
    col_apart = (point_q % LEAF_COLS - point_p % LEAF_COLS).astype(F32)
    for i, (u, v) in enumerate([(u, v) for u in (-1, 0, 1) for v in (-1, 0, 1)]):
        dr = row_apart + float(u * LEAF_ROWS)
        dc = col_apart + float(v * LEAF_COLS)
        t = jnp.sqrt(3.0 * (dr * dr + dc * dc)) / LENGTH_SCALE
        table[128 * i : 128 * i + 128] = ((1.0 + t) * jnp.exp(-t)).astype(BF16)

    fetch[2].wait()
    for l in range(top):
        for e in range(plan.ne[l]):
            wide = jnp.concatenate([downv[l, 2 * e], downv[l, 2 * e + 1]], axis=1)
            for c in range(2 * plan.ne[l + 1]):
                downst[l, 64 * c : 64 * c + 64, 128 * e : 128 * e + 128] = wide

    empty = jnp.zeros((64, 64), BF16)

    def assemble(l):
        fetch_coup[l].wait()
        for i, (dr, dc) in enumerate(plan.offsets[l]):
            for se in range(plan.ne[l]):
                for sf in (0, 1):
                    for e in range(plan.ne[l]):
                        pair = []
                        for f in (0, 1):
                            slot = SLOT_OF[e, f].get((2 * dr + se - e, 2 * dc + sf - f))
                            pair.append(empty if slot is None else coup[l][ids[l, 2 * e + f, slot]])
                        c = 2 * se + sf
                        weights[l][i, 64 * c : 64 * c + 64, 128 * e : 128 * e + 128] = jnp.concatenate(pair, axis=1)

    fetch[4].wait()
    for l in reversed(range(2, far_levels)):
        assemble(l)

    for dq in sorted(quad_steps, key=abs):
        valid = None if dq == 0 else (quad + dq >= 0) & (quad + dq < quads)
        rows = [pad + 4 * dq + (member + k) % 4 for q, k in near_partners if q == dq]
        receive(valid, [(l1.at[row], l1recv.at[row]) for row in rows])
    parts = []
    for dq in quad_steps:
        for e in (0, 1):
            for pc in (0, 1):
                row = pad + 4 * dq + 2 * e
                parts.append(jnp.concatenate([l1[row, pc], l1[row + 1, pc]], axis=1))
    lift = dot(jnp.concatenate(parts, axis=0), updup[1, 0:256])
    for i, dq in enumerate(quad_steps):
        both = []
        for e in (0, 1):
            at = 128 * i + 64 * e
            both.append(jnp.where(half32 == 0, lift[at : at + 32], lift[at + 32 : at + 64]))
        s2[i, 1] = jnp.concatenate(both, axis=1).astype(BF16)
    lift = dot(s2[quad_steps.index(0), 1], updup[2, 0:256])
    l3[quad, y] = jnp.where(half32 == y % 2, lift, 0.0).astype(BF16)
    send(None, [
        (l3.at[quad, y], l3.at[quad, y], l3recv.at[quad, y], far_device(kq, ky)) for kq, ky in far_partners
    ])
    rows_sent = slice(pad, pad + 4) if quads == 1 else slice(0, plan.window)

    def side_parts(d):
        return [
            (l1.at[rows_sent, (1 + d) // 2], l1side.at[rows_sent, side_of[d]], siderecv.at[side_of[d], 0], (g, y + d)),
            (s2.at[:, 1], s2.at[:, 1 - d], siderecv.at[side_of[d], 1], (g, y + d)),
        ]

    for d in signs:
        send(col_inside(y + d), side_parts(d))

    def adjacent(parents):
        rows = [
            jnp.concatenate([pbuf[probe_row[d], 2 * p - 1], pbuf[probe_row[d], 2 * p]], axis=1)
            for d in signs
            for p in parents
        ]
        coefs = lax.dot_general(
            jnp.concatenate(rows, axis=0), basis2[...], (((1,), (1,)), ((), ())), preferred_element_type=F32
        ).astype(BF16)
        at = 0
        for d in signs:
            for p in parents:
                s0[halo_row[d], p, :, near_half[d]] = coefs[at : at + 32]
                at += 32

    def corner_parts(d, v):
        return [
            (
                s0.at[halo_row[d], own_coef_edge[v]], s0.at[halo_row[d], coef_side[v]],
                cornerrecv.at[side_of[d], side_of[v], 0], (g, y + v),
            ),
            (
                pbuf.at[probe_row[d], own_probe_edge[v]], pbuf.at[probe_row[d], probe_side[v]],
                cornerrecv.at[side_of[d], side_of[v], 1], (g, y + v),
            ),
        ]

    for d in signs:
        receive(row_inside(g - d), arrivals(row_parts(d, 0) + row_parts(d, 1)))
    adjacent((1, 4))
    for d in signs:
        for v in signs:
            send(row_inside(g - d) & col_inside(y + v), corner_parts(d, v))

    assemble(1)
    assemble(0)

    receive(None, [
        (l3.at[row, col], l3recv.at[row, col])
        for row, col in [((quad + kq) % quads, (y + ky) % cols_dev) for kq, ky in far_partners]
    ])
    for d in signs:
        receive(col_inside(y - d), arrivals(side_parts(d) + col_parts(d)))
    for d in signs:
        receive(row_inside(g - d), arrivals(row_parts(d, 2)))
    for d in signs:
        for v in signs:
            receive(row_inside(g - d) & col_inside(y - v), arrivals(corner_parts(d, v)))
    adjacent((2, 3))

    pair_row = pad + 2 * (member // 2)
    far1 = jnp.zeros((64, 256), F32)
    for dr in (-1, 0, 1):
        row = pair_row + 2 * dr
        tiles = [
            jnp.concatenate([ref[row, at], ref[row + 1, at]], axis=1)
            for ref, at in ((l1side, 0), (l1, 0), (l1, 1), (l1side, 1))
        ]
        for dc in (-1, 0, 1):
            if (dr, dc) in plan.offsets[1]:
                lhs = jnp.concatenate([tiles[1 + dc], tiles[2 + dc]], axis=0)
                far1 = far1 + dot(lhs, weights[1][plan.offsets[1].index((dr, dc))])
    far2 = jnp.zeros((32, 256), F32)
    for i, (dr, dc) in enumerate(plan.offsets[2]):
        far2 = far2 + dot(s2[quad_steps.index(dr), 1 + dc], weights[2][i])

    for l in range(3, far_levels):
        pr_count, pc_count = plan.parents[l]
        level_top = tops[l - 3]
        if l == 3:
            for pr in range(pr_count):
                for pc in range(pc_count):
                    for e in range(plan.ne[3]):
                        level_top[1 + pr, 1 + pc, :, 128 * e : 128 * e + 128] = (
                            l3[2 * pr + e, 2 * pc] + l3[2 * pr + e, 2 * pc + 1]
                        )
        else:
            rows_below, cols_below = plan.grid[l]
            for r in range(rows_below):
                below = tops[l - 4][1 + r, 1 : 1 + cols_below].reshape(32 * cols_below, -1)
                lift = dot(below, updup[l - 1, 0 : below.shape[1]])
                for pc in range(pc_count):
                    first, second = lift[64 * pc : 64 * pc + 32], lift[64 * pc + 32 : 64 * pc + 64]
                    e = r % 2
                    level_top[1 + r // 2, 1 + pc, :, 128 * e : 128 * e + 128] = jnp.where(
                        half32 == 0, first, second
                    ).astype(BF16)

    def far_top(l):
        width = 128 * plan.ne[l]
        pr, pc = quad >> (l - 2), y >> (l - 2)
        total = jnp.zeros((32, width), F32)
        for i, (dr, dc) in enumerate(plan.offsets[l]):
            total = total + dot(tops[l - 3][1 + pr + dr, 1 + pc + dc], weights[l][i])
        return total

    local = None
    for l in reversed(range(3, far_levels)):
        total = far_top(l)
        if local is not None:
            total = total + dot(local, downst[l, 0 : local.shape[1], 0 : total.shape[1]])
        child = 2 * ((quad >> (l - 3)) % 2) + (y >> (l - 3)) % 2
        local = jnp.where(halves(total.shape) == child, total, 0.0).astype(BF16)
    total = far2 + dot(local, downst[2, 0 : local.shape[1], 0:256])
    lane = halves(total.shape)
    base = 2 * (g // 2 % 2)
    local = jnp.concatenate([jnp.where(lane == base + f, total, 0.0) for f in (0, 1)], axis=0).astype(BF16)
    total = far1 + dot(local, downst[1])
    base = 2 * (g % 2)
    local = jnp.concatenate(
        [jnp.where(lane == base + f, total[32 * pc : 32 * pc + 32], 0.0) for pc in (0, 1) for f in (0, 1)], axis=0
    ).astype(BF16)
    total = dot(local, downst[0])

    for i, (dr, dc) in enumerate(plan.offsets[0]):
        total = total + dot(s0[1 + dr, 1 + dc : 5 + dc].reshape(128, 256), weights[0][i])
    local = total.astype(BF16)
    local = jnp.concatenate([local[:, 0:128], local[:, 128:256]], axis=0)
    spread = dot(local, basis2[...])

    for e in (0, 1):
        lhs = jnp.concatenate(
            [
                pbuf[1 + e + u, 1 + v : 9 + v].reshape(256, 128)
                for u in (-1, 0, 1)
                for v in (-1, 0, 1)
            ],
            axis=1,
        )
        near = dot(lhs, table[...])
        for b in range(8):
            p, f = b // 2, b % 2
            far = spread[128 * e + 32 * p : 128 * e + 32 * p + 32, 128 * f : 128 * f + 128]
            out[e, b] = (near[32 * b : 32 * b + 32] + far).astype(BF16)

    for valid, copies in sent:

        def finish():
            for copy in copies:
                copy.wait_send()

        finish() if valid is None else pl.when(valid)(finish)


def shards(plan, probes, leaf_basis, up_transfer, down_transfer, coupling, far_ids):
    quads, cols_dev, far_levels, top = plan.quads, plan.cols_dev, plan.far_levels, plan.top
    dma = pltpu.SemaphoreType.DMA
    near_count = 4 * (1 if quads == 1 else 3) - 1
    send_count = near_count + 12 + 4 + quads * cols_dev - 1 + 4 + 8
    scratch = [
        pltpu.VMEM((4, 10, 32, 128), BF16),
        pltpu.VMEM((3, 6, 32, 256), BF16),
        pltpu.VMEM((plan.window, 2, 32, 128), BF16),
        pltpu.VMEM((plan.window, 2, 32, 128), BF16),
        pltpu.VMEM((1 if quads == 1 else 3, 3, 32, 256), BF16),
        pltpu.VMEM((quads, cols_dev, 32, 128), BF16),
        pltpu.VMEM((9 * 128, 128), BF16),
        pltpu.VMEM((64, 128), BF16),
        pltpu.SMEM(far_ids.shape, jnp.int32),
        pltpu.VMEM((128, 256), BF16),
        pltpu.VMEM((top, 4, 64, 64), BF16),
        pltpu.VMEM((top, 4, 64, 64), BF16),
        pltpu.VMEM((top, 256, 128), BF16),
        pltpu.VMEM((top, 256, 256), BF16),
    ]
    for l in range(far_levels):
        scratch.append(pltpu.VMEM((len(plan.offsets[l]), 128 * plan.ne[l], 128 * plan.ne[l]), BF16))
    scratch += [pltpu.VMEM(coupling.shape[1:], BF16) for _ in range(far_levels)]
    for l in range(3, far_levels):
        pr, pc = plan.parents[l]
        scratch.append(pltpu.VMEM((pr + 2, pc + 2, 32, 128 * plan.ne[l]), BF16))
    scratch += [
        dma((5 + far_levels,)),
        dma((send_count,)),
        dma((3, 2, 2)),
        dma((2, 2)),
        dma((2, 2, 2)),
        dma((plan.window,)),
        dma((2, 2)),
        dma((quads, cols_dev)),
    ]
    anywhere = pl.BlockSpec(memory_space=pltpu.HBM)
    vmem = pl.BlockSpec(memory_space=pltpu.VMEM)
    operands = [
        pltpu.with_memory_space_constraint(x, pltpu.HBM)
        for x in (probes, leaf_basis.T, up_transfer, down_transfer, coupling, far_ids)
    ]
    return pl.pallas_call(
        functools.partial(kernel, plan),
        out_shape=jax.ShapeDtypeStruct(probes.shape, BF16),
        in_specs=[anywhere] * 6,
        out_specs=vmem,
        scratch_shapes=scratch,
        compiler_params=pltpu.CompilerParams(
            collective_id=0, has_side_effects=True, vmem_limit_bytes=40 * 1024 * 1024
        ),
    )(*operands)


def solution(mesh):
    in_specs = (P("gx", "gy", None, None), P(), P(), P(), P(), P())
    out_specs = P("gx", "gy", None, None)

    def run(probes, leaf_basis, up_transfer, down_transfer, coupling, far_ids):
        plan = Plan(mesh.shape["gx"], mesh.shape["gy"], coupling.shape[0])
        return jax.shard_map(
            functools.partial(shards, plan), mesh=mesh, in_specs=in_specs, out_specs=out_specs, check_vma=False
        )(probes, leaf_basis, up_transfer, down_transfer, coupling, far_ids)

    return run
```
